32 devices in a mesh: gx: 8 (over y, x, core), gz: 4 (over z).
Axes of the slice: x: 2, y: 2, z: 4, core: 2. Of those that a mesh axis runs over, the one named last changes fastest.
Arguments:
- velocity: float32 [64, 3, 32, 32, 256], P(None, None, 'gx', 'gz'), may hold values from -40 to 40
- scaled_modes: float32 [64, 32, 32, 256], P(None, 'gx', 'gz'), may hold values from -70 to 70
Outputs:
- orthonormal: float32 [128, 32, 32, 256], P(None, 'gx', 'gz')
- triangle: float32 [128, 128], replicated
- lower_one: float32 [128, 128], replicated
The draws below stay inside these ranges and needn't reach their ends.
All inputs are finite; a program needn't handle non-finite values.
Results may differ from the reference program's by a relative error of at most 0.0003.
Values sent between devices are 32-bit elements; how exact they have to be, the bound alone decides.
A program may use at most 128 MiB of HBM per device.

```python
import math
import jax
import jax.numpy as jnp
from jax import lax

MODES = 64
SNAP = 64
NY = 256
COLS = 128
NX = 32
NZ = 32


def streamwise_scale(key, lowest, highest):
    position = jnp.arange(NX, dtype=jnp.float32) / NX
    rough = jax.random.uniform(key, (NX,), jnp.float32, math.log(lowest), math.log(highest))
    return jnp.exp(math.log(3.0) * position + rough)


def draw_velocity(key, part):
    first_key, second_key, third_key = jax.random.split(key, 3)
    shape = (SNAP, 3, NX, NZ, NY)
    noise = jnp.clip(jax.random.normal(first_key, shape, jnp.float32), -4.0, 4.0)
    plane = streamwise_scale(second_key, 0.6, 1.6)
    amplitude = jnp.exp(jax.random.uniform(third_key, (SNAP,), jnp.float32, math.log(0.5), math.log(2.0)))
    flow = noise * plane[None, None, :, None, None] * amplitude[:, None, None, None, None]
    return flow


def draw_scaled_modes(key, part):
    first_key, second_key, third_key, fourth_key = jax.random.split(key, 4)
    shape = (MODES, NX, NZ, NY)
    groups = (MODES + 3) // 4
    shared_shape = (groups, NX, NZ, NY)
    noise = jnp.clip(jax.random.normal(first_key, shape, jnp.float32), -4.0, 4.0)
    shared = jnp.clip(jax.random.normal(fourth_key, shared_shape, jnp.float32), -4.0, 4.0)
    plane = streamwise_scale(second_key, 0.6, 1.6)
    spread = 0.02
    column = jnp.exp(jax.random.uniform(third_key, (MODES,), jnp.float32, math.log(0.3), math.log(3.0)))
    which_shared = jnp.arange(MODES, dtype=jnp.int32) // 4
    mixed = shared[which_shared] + spread * noise
    return mixed * plane[None, :, None, None] * column[:, None, None, None]


def setup_inputs(seed: int = 0) -> dict:
    streams_of = jax.random.split(jax.random.key(seed), 3)
    velocity = draw_velocity(jax.random.fold_in(streams_of[2], 71), 0)
    scaled_modes = draw_scaled_modes(jax.random.fold_in(streams_of[2], 71), 0)
    return dict(velocity=velocity, scaled_modes=scaled_modes)


precise = lax.Precision.HIGHEST

def central(field, along):
    return (jnp.roll(field, -1, along) - jnp.roll(field, 1, along)) * 0.5

def along_wall(field):
    inner = (field[..., 2:] - field[..., :-2]) * 0.5
    bottom = (-3.0 * field[..., 0:1] + 4.0 * field[..., 1:2] - field[..., 2:3]) * 0.5
    top_side = (3.0 * field[..., -1:] - 4.0 * field[..., -2:-1] + field[..., -3:-2]) * 0.5
    return jnp.concatenate([bottom, inner, top_side], -1)

def criterion(flow):
    grad_x = central(flow, 1)
    grad_z = central(flow, 2)
    grad_y = along_wall(flow)
    diagonal_part = grad_x[0] * grad_x[0] + grad_z[1] * grad_z[1] + grad_y[2] * grad_y[2]
    cross_part = grad_z[0] * grad_x[1] + grad_y[0] * grad_x[2] + grad_y[1] * grad_z[2]
    return -0.5 * diagonal_part - cross_part

def product(left, right):
    return lax.dot_general(left, right, (((1,), (1,)), ((), ())), precision=precise)

def reference(velocity, scaled_modes):
    fields = lax.map(criterion, velocity)
    total_cells = NX * NZ * NY
    stacked = jnp.concatenate([scaled_modes.reshape(MODES, -1), fields.reshape(SNAP, -1)], 0)
    lower_one = jnp.linalg.cholesky(product(stacked, stacked) / total_cells)
    first_pass = lax.linalg.triangular_solve(lower_one, stacked, left_side=True, lower=True)
    lower_two = jnp.linalg.cholesky(product(first_pass, first_pass) / total_cells)
    basis = lax.linalg.triangular_solve(lower_two, first_pass, left_side=True, lower=True)
    triangle = jnp.dot(lower_two.T, lower_one.T, precision=precise)
    return (basis.reshape(COLS, NX, NZ, NY), triangle, lower_one)
```

```python
import functools

import jax
import jax.numpy as jnp
from jax import lax
from jax.experimental import pallas as pl
from jax.experimental.pallas import tpu as pltpu
from jax.sharding import PartitionSpec as P

MESH = pl.DeviceIdType.MESH
F32 = jnp.float32
BF16 = jnp.bfloat16
CHUNKS = 4
PIECES = 32
VMEM_LIMIT = 60 * 1024 * 1024


def split3(x):
    a = x.astype(BF16)
    rest = x - a.astype(F32)
    b = rest.astype(BF16)
    c = (rest - b.astype(F32)).astype(BF16)
    return a, b, c


def split2(x):
    a = x.astype(BF16)
    return a, (x - a.astype(F32)).astype(BF16)


def dot(x, y):
    return lax.dot_general(x, y, (((1,), (0,)), ((), ())), preferred_element_type=F32)


def dot_t(x, y):
    return lax.dot_general(x, y, (((1,), (1,)), ((), ())), preferred_element_type=F32)


def store_pieces(ref, matrix):
    rows = matrix.shape[0] // PIECES
    for i in range(PIECES):
        ref[i] = matrix[i * rows : (i + 1) * rows, :]


def lane_derivative(f):
    width = f.shape[-1]
    lane = lax.broadcasted_iota(jnp.int32, f.shape, 1)
    ahead = pltpu.roll(f, width - 1, 1)
    behind = pltpu.roll(f, 1, 1)
    ahead2 = pltpu.roll(f, width - 2, 1)
    behind2 = pltpu.roll(f, 2, 1)
    inner = ahead - behind
    bottom = -3.0 * f + 4.0 * ahead - ahead2
    top_side = 3.0 * f - 4.0 * behind + behind2
    return 0.5 * jnp.where(lane == 0, bottom, jnp.where(lane == width - 1, top_side, inner))


def halo_kernel(
    nx, nz, vel_hbm, modes_hbm, s_ref, gram_ref,
    vel, crit, modes_split, x_low, x_high, z_low, z_high, z_first, z_last, total,
    load_sem, send_sem, recv_sem,
):
    gx = lax.axis_index("gx")
    gz = lax.axis_index("gz")
    right, left = lax.rem(gx + 1, nx), lax.rem(gx + nx - 1, nx)
    front, back = lax.rem(gz + 1, nz), lax.rem(gz + nz - 1, nz)
    fields, cells_x, cells_z, width = vel_hbm.shape
    snaps = fields // 3
    modes = modes_hbm.shape[0] // (cells_x * cells_z)
    half = width // 2
    per = fields // CHUNKS
    cells = cells_x * cells_z
    group = 8 // cells_x

    def load(j):
        part = pl.ds(j * per, per)
        return pltpu.make_async_copy(vel_hbm.at[part], vel.at[part], load_sem.at[j])

    def load_modes(k):
        src = modes_hbm.at[:, pl.ds(k * half, half)]
        return pltpu.make_async_copy(src, modes_split.at[k], load_sem.at[CHUNKS + k])

    def remote(way, j):
        part = pl.ds(j * per, per)
        rows = pl.ds(j * per * cells_x, per * cells_x)
        src, dst, where = [
            (vel_hbm.at[part, cells_x - 1], x_low.at[part], (right, gz)),
            (vel_hbm.at[part, 0], x_high.at[part], (left, gz)),
            (z_last.at[rows], z_low.at[rows], (gx, front)),
            (z_first.at[rows], z_high.at[rows], (gx, back)),
        ][way]
        return pltpu.make_async_remote_copy(
            src_ref=src, dst_ref=dst, send_sem=send_sem.at[way, j], recv_sem=recv_sem.at[way, j],
            device_id=where, device_id_type=MESH,
        )

    for j in range(CHUNKS):
        load(j).start()
    for k in range(2):
        load_modes(k).start()
    barrier = pltpu.get_barrier_semaphore()
    for where in ((right, gz), (left, gz), (gx, front), (gx, back)):
        pl.semaphore_signal(barrier, inc=1, device_id=where, device_id_type=MESH)
    pl.semaphore_wait(barrier, 4)
    for j in range(CHUNKS):
        remote(0, j).start()
        remote(1, j).start()
    for j in range(CHUNKS):
        load(j).wait()

        @pl.loop(j * per // group, (j + 1) * per // group)
        def _(g):
            rows = pl.ds(pl.multiple_of(g * 8, 8), 8)
            blocks = [vel[g * group + q] for q in range(group)]
            z_first[rows, :] = jnp.concatenate([b[:, 0, :] for b in blocks], axis=0)
            z_last[rows, :] = jnp.concatenate([b[:, cells_z - 1, :] for b in blocks], axis=0)

        remote(2, j).start()
        remote(3, j).start()

    def gather(ref, c, count):
        parts = [ref.at[k][pl.ds(c, count, stride=cells), :] for k in range(2)]
        return jnp.concatenate(parts, axis=1)

    for k in range(2):
        load_modes(k).wait()
    for c in range(cells):
        s_ref[c, 0:modes, :] = gather(modes_split, c, modes)

    def snapshot(s):
        sub = lax.broadcasted_iota(jnp.int32, (cells_z, width), 0)
        u = [[vel[s * 3 + i, x] for x in range(cells_x)] for i in range(3)]
        low = [x_low[s * 3 + i] for i in range(3)]
        high = [x_high[s * 3 + i] for i in range(3)]
        for x in range(cells_x):
            gradx, gradz, grady = [], [], []
            for i in range(3):
                f = u[i][x]
                before = u[i][x - 1] if x > 0 else low[i]
                after = u[i][x + 1] if x < cells_x - 1 else high[i]
                gradx.append((after - before) * 0.5)
                row = pl.ds((s * 3 + i) * cells_x + x, 1)
                under = jnp.where(sub == 0, z_low[row, :], pltpu.roll(f, 1, 0))
                over = jnp.where(sub == cells_z - 1, z_high[row, :], pltpu.roll(f, cells_z - 1, 0))
                gradz.append((over - under) * 0.5)
                grady.append(lane_derivative(f))
            diagonal_part = gradx[0] * gradx[0] + gradz[1] * gradz[1] + grady[2] * grady[2]
            cross_part = gradz[0] * gradx[1] + grady[0] * gradx[2] + grady[1] * gradz[2]
            place = pl.multiple_of((s * cells_x + x) * cells_z, cells_z)
            value = -0.5 * diagonal_part - cross_part
            for k in range(2):
                crit[k, pl.ds(place, cells_z), :] = value[:, k * half : (k + 1) * half]

    for j in range(CHUNKS):
        for way in range(4):
            remote(way, j).wait_recv()

        @pl.loop(j * snaps // CHUNKS, (j + 1) * snaps // CHUNKS)
        def _(s):
            snapshot(s)

    for j in range(CHUNKS):
        for way in range(4):
            remote(way, j).wait_send()

    for c in range(cells):
        s_ref[c, modes:, :] = gather(crit, c, snaps)

    total[...] = jnp.zeros_like(total)

    @pl.loop(0, cells)
    def _(c):
        a, b, d = split3(s_ref[c])
        total[0] += dot_t(a, a) + dot_t(b, b)
        total[1] += dot_t(jnp.concatenate([b, d], axis=1), jnp.concatenate([a, a], axis=1))

    cross = total[1]
    store_pieces(gram_ref, total[0] + (cross + cross.T))


def halo_call(velocity, scaled_modes, nx, nz):
    snaps, _, cells_x, cells_z, width = velocity.shape
    modes = scaled_modes.shape[0]
    fields = snaps * 3
    cells = cells_x * cells_z
    columns = modes + snaps
    x_face = pltpu.VMEM((fields, cells_z, width), F32)
    z_face = pltpu.VMEM((fields * cells_x, width), F32)
    return pl.pallas_call(
        functools.partial(halo_kernel, nx, nz),
        out_shape=(
            jax.ShapeDtypeStruct((cells, columns, width), F32),
            jax.ShapeDtypeStruct((PIECES, columns // PIECES, columns), F32),
        ),
        in_specs=[pl.BlockSpec(memory_space=pl.ANY)] * 2,
        out_specs=[pl.BlockSpec(memory_space=pltpu.VMEM)] * 2,
        scratch_shapes=[
            pltpu.VMEM((fields, cells_x, cells_z, width), F32),
            pltpu.VMEM((2, snaps * cells, width // 2), F32),
            pltpu.VMEM((2, modes * cells, width // 2), F32),
            x_face, x_face, z_face, z_face, z_face, z_face,
            pltpu.VMEM((2, columns, columns), F32),
            pltpu.SemaphoreType.DMA((CHUNKS + 2,)),
            pltpu.SemaphoreType.DMA((4, CHUNKS)),
            pltpu.SemaphoreType.DMA((4, CHUNKS)),
        ],
        compiler_params=pltpu.CompilerParams(
            collective_id=0, has_side_effects=True, vmem_limit_bytes=VMEM_LIMIT
        ),
        name="halo_criterion_gram",
    )(velocity.reshape(fields, cells_x, cells_z, width), scaled_modes.reshape(modes * cells, width))


def reduce_kernel(nx, nz, part_ref, sum_ref, inbox, send_sem, recv_sem, send_two, recv_two):
    count = nx * nz
    owners = min(count, PIECES)
    me = lax.axis_index("gx") * nz + lax.axis_index("gz")

    def place(k):
        return (lax.div(k, nz), lax.rem(k, nz))

    def other(step):
        return lax.rem(me + step, count)

    barrier = pltpu.get_barrier_semaphore()

    @pl.loop(1, count)
    def _(step):
        pl.semaphore_signal(barrier, inc=1, device_id=place(other(step)), device_id_type=MESH)

    pl.semaphore_wait(barrier, count - 1)

    def scatter(k):
        return pltpu.make_async_remote_copy(
            src_ref=part_ref.at[k], dst_ref=inbox.at[me], send_sem=send_sem, recv_sem=recv_sem,
            device_id=place(k), device_id_type=MESH,
        )

    def spread(k):
        return pltpu.make_async_remote_copy(
            src_ref=sum_ref.at[me], dst_ref=sum_ref.at[me], send_sem=send_two, recv_sem=recv_two,
            device_id=place(k), device_id_type=MESH,
        )

    def wait_bytes(ref, number, sem):
        if number:
            view = ref.at[pl.ds(0, number)]
            pltpu.make_async_copy(view, view, sem).wait()

    if owners == count:

        @pl.loop(1, count)
        def _(step):
            scatter(other(step)).start()

        inbox[me] = part_ref[me]
        wait_bytes(inbox, count - 1, recv_sem)
        sum_ref[me] = jnp.sum(inbox[...], axis=0)

        @pl.loop(1, count)
        def _(step):
            spread(other(step)).start()

        wait_bytes(sum_ref, count - 1, recv_two)
        wait_bytes(inbox, count - 1, send_sem)
        wait_bytes(inbox, count - 1, send_two)
    else:
        owner = me < owners

        @pl.loop(0, owners)
        def _(k):
            @pl.when(k != me)
            def _():
                scatter(k).start()

        @pl.when(owner)
        def _():
            inbox[me] = part_ref[me]
            wait_bytes(inbox, count - 1, recv_sem)
            sum_ref[me] = jnp.sum(inbox[...], axis=0)

            @pl.loop(1, count)
            def _(step):
                spread(other(step)).start()

            wait_bytes(sum_ref, owners - 1, recv_two)
            wait_bytes(inbox, owners - 1, send_sem)
            wait_bytes(inbox, count - 1, send_two)

        @pl.when(jnp.logical_not(owner))
        def _():
            wait_bytes(sum_ref, owners, recv_two)
            wait_bytes(inbox, owners, send_sem)


def reduce_call(parts, nx, nz, ident):
    pieces, rows, columns = parts.shape
    return pl.pallas_call(
        functools.partial(reduce_kernel, nx, nz),
        out_shape=jax.ShapeDtypeStruct(parts.shape, F32),
        in_specs=[pl.BlockSpec(memory_space=pltpu.VMEM)],
        out_specs=pl.BlockSpec(memory_space=pltpu.VMEM),
        scratch_shapes=[
            pltpu.VMEM((nx * nz, rows, columns), F32),
            pltpu.SemaphoreType.DMA, pltpu.SemaphoreType.DMA,
            pltpu.SemaphoreType.DMA, pltpu.SemaphoreType.DMA,
        ],
        compiler_params=pltpu.CompilerParams(
            collective_id=ident, has_side_effects=True, vmem_limit_bytes=VMEM_LIMIT
        ),
        name="gram_reduce",
    )(parts)


def factor(tiles, upper_ref, inverse_ref, block=4):
    size = tiles[0].shape[1]
    lane = lax.broadcasted_iota(jnp.int32, (1, size), 1)
    sub = lax.broadcasted_iota(jnp.int32, (8, size), 0)
    for k in range(0, size, block):
        home = k // 8
        off = k % 8
        tile = tiles[home]
        rows = [tile[off + i : off + i + 1, :] for i in range(block)]
        pivot = [
            [tile[off + i : off + i + 1, k + j : k + j + 1] for j in range(block)]
            for i in range(block)
        ]
        inv = []
        for i in range(block):
            inv.append(1.0 / pivot[i][i])
            fixed = jnp.where(lane == k + i, 1.0, rows[i])
            scale = jnp.sqrt(inv[i])
            upper_ref[k + i : k + i + 1, :] = jnp.where(lane >= k + i, rows[i] * scale, 0.0)
            inverse_ref[k + i : k + i + 1, :] = jnp.where(lane <= k + i, fixed * scale, 0.0)
            for j in range(i + 1, block):
                ratio = pivot[i][j] * inv[i]
                rows[j] = jnp.where(lane == k + i, 0.0, rows[j]) - ratio * fixed
                for m in range(j, block):
                    pivot[j][m] = pivot[j][m] - ratio * pivot[i][m]
            rows[i] = fixed
        inside = (lane >= k) & (lane < k + block)
        clear = [jnp.where(inside & (lane > k + i), 0.0, rows[i]) for i in range(block)]
        first = home if off + block < 8 else home + 1
        for t in range(first, len(tiles)):
            tile = tiles[t]
            new = jnp.where(inside, 0.0, tile)
            weights = []
            for i in range(block):
                entry = tile[:, k + i : k + i + 1]
                for m in range(i):
                    entry = entry - weights[m] * pivot[m][i]
                weights.append(entry * inv[i])
                new = new - weights[i] * clear[i]
            tiles[t] = jnp.where(sub >= off + block, new, tile) if t == home else new


def load_tiles(sum_ref, scale):
    rows = sum_ref.shape[1]
    step = 8 // rows
    return [
        jnp.concatenate([sum_ref[t * step + q] for q in range(step)], axis=0) * scale
        for t in range(sum_ref.shape[0] // step)
    ]


def factor_one_kernel(scale, sum_ref, lower_ref, upper_ref, inverse_ref):
    factor(load_tiles(sum_ref, scale), upper_ref, inverse_ref)
    lower_ref[...] = upper_ref[...].T


def factor_two_kernel(scale, sum_ref, upper_one_ref, triangle_ref, inverse_ref, upper_ref):
    factor(load_tiles(sum_ref, scale), upper_ref, inverse_ref)
    triangle_ref[...] = lax.dot_general(
        upper_ref[...], upper_one_ref[...], (((1,), (0,)), ((), ())),
        precision=lax.Precision.HIGHEST, preferred_element_type=F32,
    )


def first_kernel(s_ref, inverse_ref, x_ref, gram_ref, total):
    step = pl.program_id(0)
    wa, wb, wc = split3(inverse_ref[...])
    w_one = jnp.concatenate([wa, wa], axis=1)
    w_two = jnp.concatenate([wb, wb], axis=1)
    w_three = jnp.concatenate([wa, wc], axis=1)

    @pl.when(step == 0)
    def _():
        total[...] = jnp.zeros_like(total)

    same, cross = total[0], total[1]
    for c in range(s_ref.shape[0]):
        sa, sb, sc = split3(s_ref[c])
        pair = jnp.concatenate([sa, sb], axis=0)
        ends = jnp.concatenate([sc, sa], axis=0)
        x = dot(w_one, pair) + (dot(w_two, pair) + dot(w_three, ends))
        x_ref[c] = x
        a, b = split2(x)
        same = same + dot_t(a, a)
        cross = cross + dot_t(b, a)
    total[0] = same
    total[1] = cross

    @pl.when(step == pl.num_programs(0) - 1)
    def _():
        store_pieces(gram_ref, total[0] + (total[1] + total[1].T))


def second_kernel(x_ref, inverse_ref, out_ref):
    wa, wb = split2(inverse_ref[...])
    w_all = jnp.concatenate([wa, wa, wb], axis=1)
    columns, _, width = out_ref.shape
    for c in range(x_ref.shape[0]):
        a, b = split2(x_ref[c])
        out_ref[:, c, :] = dot(w_all, jnp.concatenate([a, b, a], axis=0))


def shards(velocity, scaled_modes):
    snaps, _, cells_x, cells_z, width = velocity.shape
    columns = scaled_modes.shape[0] + snaps
    nx, nz = lax.axis_size("gx"), lax.axis_size("gz")
    cells = cells_x * cells_z
    scale = 1.0 / (cells * nx * nz * width)
    square = jax.ShapeDtypeStruct((columns, columns), F32)
    whole = pl.BlockSpec(memory_space=pltpu.VMEM)
    params = pltpu.CompilerParams(vmem_limit_bytes=VMEM_LIMIT)

    stacked, part_one = halo_call(velocity, scaled_modes, nx, nz)
    sum_one = reduce_call(part_one, nx, nz, 1)
    lower_one, upper_one, inverse_one = pl.pallas_call(
        functools.partial(factor_one_kernel, scale),
        out_shape=(square, square, square), in_specs=[whole], out_specs=[whole] * 3,
        compiler_params=params, name="factor_one",
    )(sum_one)
    group = 4
    block = pl.BlockSpec((group, columns, width), lambda i: (i, 0, 0))
    still = pl.BlockSpec((columns, columns), lambda i: (0, 0))
    first_pass, part_two = pl.pallas_call(
        first_kernel,
        grid=(cells // group,),
        out_shape=(
            jax.ShapeDtypeStruct(stacked.shape, F32),
            jax.ShapeDtypeStruct(part_one.shape, F32),
        ),
        in_specs=[block, still],
        out_specs=[block, pl.BlockSpec(part_one.shape, lambda i: (0, 0, 0))],
        scratch_shapes=[pltpu.VMEM((2, columns, columns), F32)],
        compiler_params=params, name="first_pass",
    )(stacked, inverse_one)
    sum_two = reduce_call(part_two, nx, nz, 2)
    triangle, inverse_two = pl.pallas_call(
        functools.partial(factor_two_kernel, scale),
        out_shape=(square, square), in_specs=[whole] * 2, out_specs=[whole] * 2,
        scratch_shapes=[pltpu.VMEM((columns, columns), F32)],
        compiler_params=params, name="factor_two",
    )(sum_two, upper_one)
    basis = pl.pallas_call(
        second_kernel,
        grid=(cells_x,),
        out_shape=jax.ShapeDtypeStruct((columns, cells, width), F32),
        in_specs=[pl.BlockSpec((cells_z, columns, width), lambda i: (i, 0, 0)), still],
        out_specs=pl.BlockSpec((columns, cells_z, width), lambda i: (0, i, 0)),
        compiler_params=params, name="second_pass",
    )(first_pass, inverse_two)
    return (basis.reshape(columns, cells_x, cells_z, width), triangle, lower_one)


def solution(mesh):
    in_specs = (P(None, None, "gx", "gz", None), P(None, "gx", "gz", None))
    out_specs = (P(None, "gx", "gz", None), P(), P())
    return jax.shard_map(shards, mesh=mesh, in_specs=in_specs, out_specs=out_specs, check_vma=False)
```

```python
import functools

import jax
import jax.numpy as jnp
from jax import lax
from jax.experimental import pallas as pl
from jax.experimental.pallas import tpu as pltpu
from jax.sharding import PartitionSpec as P

MESH = pl.DeviceIdType.MESH
F32 = jnp.float32
BF16 = jnp.bfloat16
CHUNKS = 8
PIECES = 32
VMEM_LIMIT = 60 * 1024 * 1024


def split3(x):
    a = x.astype(BF16)
    rest = x - a.astype(F32)
    b = rest.astype(BF16)
    c = (rest - b.astype(F32)).astype(BF16)
    return a, b, c


def split2(x):
    a = x.astype(BF16)
    return a, (x - a.astype(F32)).astype(BF16)


def dot(x, y):
    return lax.dot_general(x, y, (((1,), (0,)), ((), ())), preferred_element_type=F32)


def dot_t(x, y):
    return lax.dot_general(x, y, (((1,), (1,)), ((), ())), preferred_element_type=F32)


def store_pieces(ref, matrix):
    rows = matrix.shape[0] // PIECES
    for i in range(PIECES):
        ref[i] = matrix[i * rows : (i + 1) * rows, :]


def lane_derivative(f):
    width = f.shape[-1]
    lane = lax.broadcasted_iota(jnp.int32, f.shape, 1)
    ahead = pltpu.roll(f, width - 1, 1)
    behind = pltpu.roll(f, 1, 1)
    ahead2 = pltpu.roll(f, width - 2, 1)
    behind2 = pltpu.roll(f, 2, 1)
    inner = ahead - behind
    bottom = -3.0 * f + 4.0 * ahead - ahead2
    top_side = 3.0 * f - 4.0 * behind + behind2
    return 0.5 * jnp.where(lane == 0, bottom, jnp.where(lane == width - 1, top_side, inner))


def halo_kernel(
    nx, nz, vel_hbm, modes_hbm, s_ref, sum_ref,
    vel, crit, modes_split, x_low, x_high, z_low, z_high, z_first, z_last, total,
    load_sem, send_sem, recv_sem, part, inbox, reduce_sems,
):
    gx = lax.axis_index("gx")
    gz = lax.axis_index("gz")
    right, left = lax.rem(gx + 1, nx), lax.rem(gx + nx - 1, nx)
    front, back = lax.rem(gz + 1, nz), lax.rem(gz + nz - 1, nz)
    fields, cells_x, cells_z, width = vel_hbm.shape
    snaps = fields // 3
    modes = modes_hbm.shape[0] // (cells_x * cells_z)
    half = width // 2
    per = fields // CHUNKS
    cells = cells_x * cells_z
    group = 8 // cells_x

    def load(j):
        part = pl.ds(j * per, per)
        return pltpu.make_async_copy(vel_hbm.at[part], vel.at[part], load_sem.at[j])

    def load_modes(k):
        src = modes_hbm.at[:, pl.ds(k * half, half)]
        return pltpu.make_async_copy(src, modes_split.at[k], load_sem.at[CHUNKS + k])

    def remote(way, j):
        part = pl.ds(j * per, per)
        rows = pl.ds(j * per * cells_x, per * cells_x)
        src, dst, where = [
            (vel_hbm.at[part, cells_x - 1], x_low.at[part], (right, gz)),
            (vel_hbm.at[part, 0], x_high.at[part], (left, gz)),
            (z_last.at[rows], z_low.at[rows], (gx, front)),
            (z_first.at[rows], z_high.at[rows], (gx, back)),
        ][way]
        return pltpu.make_async_remote_copy(
            src_ref=src, dst_ref=dst, send_sem=send_sem.at[way, j], recv_sem=recv_sem.at[way, j],
            device_id=where, device_id_type=MESH,
        )

    greet(nx, nz)
    for j in range(CHUNKS):
        load(j).start()
    for k in range(2):
        load_modes(k).start()
    pl.semaphore_wait(pltpu.get_barrier_semaphore(), nx * nz - 1)
    for j in range(CHUNKS):
        remote(0, j).start()
        remote(1, j).start()
    for j in range(CHUNKS):
        load(j).wait()

        @pl.loop(j * per // group, (j + 1) * per // group)
        def _(g):
            rows = pl.ds(pl.multiple_of(g * 8, 8), 8)
            blocks = [vel[g * group + q] for q in range(group)]
            z_first[rows, :] = jnp.concatenate([b[:, 0, :] for b in blocks], axis=0)
            z_last[rows, :] = jnp.concatenate([b[:, cells_z - 1, :] for b in blocks], axis=0)

        remote(2, j).start()
        remote(3, j).start()

    def gather(ref, c, count):
        parts = [ref.at[k][pl.ds(c, count, stride=cells), :] for k in range(2)]
        return jnp.concatenate(parts, axis=1)

    for k in range(2):
        load_modes(k).wait()
    for c in range(cells):
        s_ref[c, 0:modes, :] = gather(modes_split, c, modes)

    def snapshot(s):
        sub = lax.broadcasted_iota(jnp.int32, (cells_z, width), 0)
        u = [[vel[s * 3 + i, x] for x in range(cells_x)] for i in range(3)]
        low = [x_low[s * 3 + i] for i in range(3)]
        high = [x_high[s * 3 + i] for i in range(3)]
        for x in range(cells_x):
            gradx, gradz, grady = [], [], []
            for i in range(3):
                f = u[i][x]
                before = u[i][x - 1] if x > 0 else low[i]
                after = u[i][x + 1] if x < cells_x - 1 else high[i]
                gradx.append((after - before) * 0.5)
                row = pl.ds((s * 3 + i) * cells_x + x, 1)
                under = jnp.where(sub == 0, z_low[row, :], pltpu.roll(f, 1, 0))
                over = jnp.where(sub == cells_z - 1, z_high[row, :], pltpu.roll(f, cells_z - 1, 0))
                gradz.append((over - under) * 0.5)
                grady.append(lane_derivative(f))
            diagonal_part = gradx[0] * gradx[0] + gradz[1] * gradz[1] + grady[2] * grady[2]
            cross_part = gradz[0] * gradx[1] + grady[0] * gradx[2] + grady[1] * gradz[2]
            place = pl.multiple_of((s * cells_x + x) * cells_z, cells_z)
            value = -0.5 * diagonal_part - cross_part
            for k in range(2):
                crit[k, pl.ds(place, cells_z), :] = value[:, k * half : (k + 1) * half]

    few = snaps // CHUNKS
    for j in range(CHUNKS):
        for way in range(4):
            remote(way, j).wait_recv()

        @pl.loop(j * few, (j + 1) * few)
        def _(s):
            snapshot(s)

        for c in range(cells):
            got = [crit.at[k][pl.ds(j * few * cells + c, few, stride=cells), :] for k in range(2)]
            s_ref[c, modes + j * few : modes + (j + 1) * few, :] = jnp.concatenate(got, axis=1)

    total[...] = jnp.zeros_like(total)
    columns = s_ref.shape[1]

    @pl.loop(0, cells // 4)
    def _(g):
        pieces = [split3(s_ref[g * 4 + q]) for q in range(4)]
        a, b, d = [jnp.concatenate(kind, axis=1) for kind in zip(*pieces)]
        total[0:columns] += dot_t(b, b)
        total[columns:] += dot_t(jnp.concatenate([a, b, d], axis=0), a)

    cross = total[2 * columns : 3 * columns] + total[3 * columns :]
    store_pieces(part, total[columns : 2 * columns] + (total[0:columns] + (cross + cross.T)))
    for j in range(CHUNKS):
        for way in range(4):
            remote(way, j).wait_send()
    reduce_all(nx, nz, part, sum_ref, inbox, reduce_sems)


def halo_call(velocity, scaled_modes, nx, nz):
    snaps, _, cells_x, cells_z, width = velocity.shape
    modes = scaled_modes.shape[0]
    fields = snaps * 3
    cells = cells_x * cells_z
    columns = modes + snaps
    x_face = pltpu.VMEM((fields, cells_z, width), F32)
    z_face = pltpu.VMEM((fields * cells_x, width), F32)
    return pl.pallas_call(
        functools.partial(halo_kernel, nx, nz),
        out_shape=(
            jax.ShapeDtypeStruct((cells, columns, width), F32),
            jax.ShapeDtypeStruct((PIECES, columns // PIECES, columns), F32),
        ),
        in_specs=[pl.BlockSpec(memory_space=pl.ANY)] * 2,
        out_specs=[pl.BlockSpec(memory_space=pltpu.VMEM)] * 2,
        scratch_shapes=[
            pltpu.VMEM((fields, cells_x, cells_z, width), F32),
            pltpu.VMEM((2, snaps * cells, width // 2), F32),
            pltpu.VMEM((2, modes * cells, width // 2), F32),
            x_face, x_face, z_face, z_face, z_face, z_face,
            pltpu.VMEM((4 * columns, columns), F32),
            pltpu.SemaphoreType.DMA((CHUNKS + 2,)),
            pltpu.SemaphoreType.DMA((4, CHUNKS)),
            pltpu.SemaphoreType.DMA((4, CHUNKS)),
            *reduce_scratch(nx * nz, columns),
        ],
        compiler_params=pltpu.CompilerParams(
            collective_id=0, has_side_effects=True, vmem_limit_bytes=VMEM_LIMIT
        ),
        name="halo_criterion_gram",
    )(velocity.reshape(fields, cells_x, cells_z, width), scaled_modes.reshape(modes * cells, width))


def greet(nx, nz):
    gx, gz = lax.axis_index("gx"), lax.axis_index("gz")
    barrier = pltpu.get_barrier_semaphore()
    for dx, dz in other_steps(nx, nz):
        where = (lax.rem(gx + dx, nx), lax.rem(gz + dz, nz))
        pl.semaphore_signal(barrier, inc=1, device_id=where, device_id_type=MESH)


def other_steps(nx, nz):
    return [(dx, dz) for dx in range(nx) for dz in range(nz) if dx or dz]


def reduce_all(nx, nz, part_ref, sum_ref, inbox, sems):
    send_sem, recv_sem, send_two, recv_two = [sems.at[i] for i in range(4)]
    count = nx * nz
    owners = min(count, PIECES)
    gx, gz = lax.axis_index("gx"), lax.axis_index("gz")
    me = gx * nz + gz

    def target(dx, dz):
        return lax.rem(gx + dx, nx), lax.rem(gz + dz, nz)

    def scatter(where):
        return pltpu.make_async_remote_copy(
            src_ref=part_ref.at[where[0] * nz + where[1]], dst_ref=inbox.at[me],
            send_sem=send_sem, recv_sem=recv_sem, device_id=where, device_id_type=MESH,
        )

    def spread(where):
        return pltpu.make_async_remote_copy(
            src_ref=sum_ref.at[me], dst_ref=sum_ref.at[me], send_sem=send_two, recv_sem=recv_two,
            device_id=where, device_id_type=MESH,
        )

    def wait_bytes(ref, number, sem):
        if number:
            view = ref.at[pl.ds(0, number)]
            pltpu.make_async_copy(view, view, sem).wait()

    def add_up():
        inbox[me] = part_ref[me]
        wait_bytes(inbox, count - 1, recv_sem)
        sum_ref[me] = jnp.sum(inbox[...], axis=0)

    if owners == count:
        for step in other_steps(nx, nz):
            scatter(target(*step)).start()
        add_up()
        for step in other_steps(nx, nz):
            spread(target(*step)).start()
        wait_bytes(sum_ref, count - 1, recv_two)
        wait_bytes(inbox, count - 1, send_sem)
        wait_bytes(inbox, count - 1, send_two)
    else:
        owner = me < owners

        @pl.loop(0, owners)
        def _(k):
            @pl.when(k != me)
            def _():
                scatter((lax.div(k, nz), lax.rem(k, nz))).start()

        @pl.when(owner)
        def _():
            add_up()

            @pl.loop(1, count)
            def _(step):
                k = lax.rem(me + step, count)
                spread((lax.div(k, nz), lax.rem(k, nz))).start()

            wait_bytes(sum_ref, owners - 1, recv_two)
            wait_bytes(inbox, owners - 1, send_sem)
            wait_bytes(inbox, count - 1, send_two)

        @pl.when(jnp.logical_not(owner))
        def _():
            wait_bytes(sum_ref, owners, recv_two)
            wait_bytes(inbox, owners, send_sem)


def reduce_scratch(count, columns):
    rows = columns // PIECES
    return [
        pltpu.VMEM((PIECES, rows, columns), F32),
        pltpu.VMEM((count, rows, columns), F32),
        pltpu.SemaphoreType.DMA((4,)),
    ]


def factor(tiles, upper_ref, inverse_ref):
    size = tiles[0].shape[1]
    shape = (8, size)
    lane = lax.broadcasted_iota(jnp.int32, shape, 1)
    sub = lax.broadcasted_iota(jnp.int32, shape, 0)
    for home in range(len(tiles)):
        k = home * 8
        tile = tiles[home]
        rows = [jnp.broadcast_to(tile[i : i + 1, :], shape) for i in range(8)]
        pivot = [
            [jnp.broadcast_to(rows[i][:, k + j : k + j + 1], shape) if j >= i else None for j in range(8)]
            for i in range(8)
        ]
        inv = []
        upper = jnp.zeros(shape, F32)
        inverse = jnp.zeros(shape, F32)
        for i in range(8):
            inv.append(1.0 / pivot[i][i])
            fixed = jnp.where(lane == k + i, 1.0, rows[i])
            scale = jnp.sqrt(inv[i])
            upper = jnp.where((sub == i) & (lane >= k + i), rows[i] * scale, upper)
            inverse = jnp.where((sub == i) & (lane <= k + i), fixed * scale, inverse)
            for j in range(i + 1, 8):
                ratio = pivot[i][j] * inv[i]
                rows[j] = jnp.where(lane == k + i, 0.0, rows[j]) - ratio * fixed
                for m in range(j, 8):
                    pivot[j][m] = pivot[j][m] - ratio * pivot[i][m]
            rows[i] = fixed
        upper_ref[k : k + 8, :] = upper
        inverse_ref[k : k + 8, :] = inverse
        inside = (lane >= k) & (lane < k + 8)
        clear = [jnp.where(inside & (lane > k + i), 0.0, rows[i]) for i in range(8)]
        for t in range(home + 1, len(tiles)):
            tile = tiles[t]
            new = jnp.where(inside, 0.0, tile)
            weights = []
            for i in range(8):
                entry = jnp.broadcast_to(tile[:, k + i : k + i + 1], shape)
                for m in range(i):
                    entry = entry - weights[m] * pivot[m][i]
                weights.append(entry * inv[i])
                new = new - weights[i] * clear[i]
            tiles[t] = new


def load_tiles(sum_ref, scale):
    rows = sum_ref.shape[1]
    step = 8 // rows
    return [
        jnp.concatenate([sum_ref[t * step + q] for q in range(step)], axis=0) * scale
        for t in range(sum_ref.shape[0] // step)
    ]


def factor_one_kernel(scale, sum_ref, lower_ref, upper_ref, inverse_ref):
    factor(load_tiles(sum_ref, scale), upper_ref, inverse_ref)
    lower_ref[...] = upper_ref[...].T


def first_kernel(nx, nz, s_ref, inverse_ref, x_ref, sum_ref, total, part, inbox, reduce_sems):
    greet(nx, nz)
    wa, wb, wc = split3(inverse_ref[...])
    columns = wa.shape[0]
    main = jnp.concatenate(
        [
            jnp.concatenate([wa, wa], axis=1),
            jnp.concatenate([wb, wb], axis=1),
            jnp.concatenate([wc, jnp.zeros_like(wc)], axis=1),
        ],
        axis=0,
    )
    total[...] = jnp.zeros_like(total)

    @pl.loop(0, s_ref.shape[0] // 4)
    def _(g):
        high, low = [], []
        for q in range(4):
            sa, sb, sc = split3(s_ref[g * 4 + q])
            y = dot(main, jnp.concatenate([sa, sb], axis=0))
            x = y[0:columns] + (y[columns : 2 * columns] + y[2 * columns :] + dot(wa, sc))
            x_ref[g * 4 + q] = x
            a, b = split2(x)
            high.append(a)
            low.append(b)
        a = jnp.concatenate(high, axis=1)
        total[...] += dot_t(jnp.concatenate([a, jnp.concatenate(low, axis=1)], axis=0), a)

    cross = total[columns:]
    store_pieces(part, total[0:columns] + (cross + cross.T))
    pl.semaphore_wait(pltpu.get_barrier_semaphore(), nx * nz - 1)
    reduce_all(nx, nz, part, sum_ref, inbox, reduce_sems)


def second_kernel(
    scale, x_ref, sum_ref, upper_one_ref, out_ref, triangle_ref, inverse_ref, upper_ref
):
    @pl.when(pl.program_id(0) == 0)
    def _():
        factor(load_tiles(sum_ref, scale), upper_ref, inverse_ref)
        triangle_ref[...] = lax.dot_general(
            upper_ref[...], upper_one_ref[...], (((1,), (0,)), ((), ())),
            precision=lax.Precision.HIGHEST, preferred_element_type=F32,
        )

    wa, wb = split2(inverse_ref[...])
    columns, _, width = out_ref.shape
    both = jnp.concatenate(
        [jnp.concatenate([wa, wa], axis=1), jnp.concatenate([wb, jnp.zeros_like(wb)], axis=1)],
        axis=0,
    )
    for c in range(x_ref.shape[0]):
        y = dot(both, jnp.concatenate(split2(x_ref[c]), axis=0))
        out_ref[:, c, :] = y[0:columns] + y[columns:]


def shards(velocity, scaled_modes):
    snaps, _, cells_x, cells_z, width = velocity.shape
    columns = scaled_modes.shape[0] + snaps
    nx, nz = lax.axis_size("gx"), lax.axis_size("gz")
    cells = cells_x * cells_z
    scale = 1.0 / (cells * nx * nz * width)
    square = jax.ShapeDtypeStruct((columns, columns), F32)
    whole = pl.BlockSpec(memory_space=pltpu.VMEM)
    params = pltpu.CompilerParams(vmem_limit_bytes=VMEM_LIMIT)

    stacked, sum_one = halo_call(velocity, scaled_modes, nx, nz)
    lower_one, upper_one, inverse_one = pl.pallas_call(
        functools.partial(factor_one_kernel, scale),
        out_shape=(square, square, square), in_specs=[whole], out_specs=[whole] * 3,
        compiler_params=params, name="factor_one",
    )(sum_one)
    first_pass, sum_two = pl.pallas_call(
        functools.partial(first_kernel, nx, nz),
        out_shape=(
            jax.ShapeDtypeStruct(stacked.shape, F32),
            jax.ShapeDtypeStruct(sum_one.shape, F32),
        ),
        in_specs=[whole] * 2,
        out_specs=[whole] * 2,
        scratch_shapes=[
            pltpu.VMEM((2 * columns, columns), F32), *reduce_scratch(nx * nz, columns)
        ],
        compiler_params=pltpu.CompilerParams(
            collective_id=1, has_side_effects=True, vmem_limit_bytes=VMEM_LIMIT
        ),
        name="first_pass_gram",
    )(stacked, inverse_one)
    still = pl.BlockSpec((columns, columns), lambda i: (0, 0))
    basis, triangle = pl.pallas_call(
        functools.partial(second_kernel, scale),
        grid=(cells_x,),
        out_shape=(jax.ShapeDtypeStruct((columns, cells, width), F32), square),
        in_specs=[
            pl.BlockSpec((cells_z, columns, width), lambda i: (i, 0, 0)),
            pl.BlockSpec(sum_two.shape, lambda i: (0, 0, 0)),
            still,
        ],
        out_specs=[pl.BlockSpec((columns, cells_z, width), lambda i: (0, i, 0)), still],
        scratch_shapes=[pltpu.VMEM((columns, columns), F32)] * 2,
        compiler_params=params, name="second_pass",
    )(first_pass, sum_two, upper_one)
    return (basis.reshape(columns, cells_x, cells_z, width), triangle, lower_one)


def solution(mesh):
    in_specs = (P(None, None, "gx", "gz", None), P(None, "gx", "gz", None))
    out_specs = (P(None, "gx", "gz", None), P(), P())
    return jax.shard_map(shards, mesh=mesh, in_specs=in_specs, out_specs=out_specs, check_vma=False)
```

```python
import functools

import jax
import jax.numpy as jnp
from jax import lax
from jax.experimental import pallas as pl
from jax.experimental.pallas import tpu as pltpu
from jax.sharding import PartitionSpec as P

MESH = pl.DeviceIdType.MESH
F32 = jnp.float32
BF16 = jnp.bfloat16
CHUNKS = 8
WINDOW = 3
GROUP = 8
PIECES = 32
VMEM_LIMIT = 60 * 1024 * 1024


def split3(x):
    a = x.astype(BF16)
    rest = x - a.astype(F32)
    b = rest.astype(BF16)
    c = (rest - b.astype(F32)).astype(BF16)
    return a, b, c


def split2(x):
    a = x.astype(BF16)
    return a, (x - a.astype(F32)).astype(BF16)


def dot(x, y):
    return lax.dot_general(x, y, (((1,), (0,)), ((), ())), preferred_element_type=F32)


def dot_t(x, y):
    return lax.dot_general(x, y, (((1,), (1,)), ((), ())), preferred_element_type=F32)


def store_pieces(ref, matrix):
    rows = matrix.shape[0] // PIECES
    for i in range(PIECES):
        ref[i] = matrix[i * rows : (i + 1) * rows, :]


def lane_derivative(f):
    width = f.shape[-1]
    lane = lax.broadcasted_iota(jnp.int32, f.shape, 1)
    ahead = pltpu.roll(f, width - 1, 1)
    behind = pltpu.roll(f, 1, 1)
    ahead2 = pltpu.roll(f, width - 2, 1)
    behind2 = pltpu.roll(f, 2, 1)
    inner = ahead - behind
    bottom = -3.0 * f + 4.0 * ahead - ahead2
    top_side = 3.0 * f - 4.0 * behind + behind2
    return 0.5 * jnp.where(lane == 0, bottom, jnp.where(lane == width - 1, top_side, inner))


def halo_kernel(
    nx, nz, scale, vel_hbm, modes_hbm, x_hbm, sum_two_ref, upper_ref,
    s_ref, x_ref, inverse_ref, sum_ref, vel, crit, modes_split, x_low, x_high, z_low, z_high, z_first, z_last, total,
    load_sem, send_sem, recv_sem, part, inbox, reduce_sems, part_two, inbox_two, reduce_two,
):
    gx = lax.axis_index("gx")
    gz = lax.axis_index("gz")
    right, left = lax.rem(gx + 1, nx), lax.rem(gx + nx - 1, nx)
    front, back = lax.rem(gz + 1, nz), lax.rem(gz + nz - 1, nz)
    fields, cells_x, cells_z, width = vel_hbm.shape
    snaps = fields // 3
    modes = modes_hbm.shape[0] // (cells_x * cells_z)
    half = width // 2
    per = fields // CHUNKS
    cells = cells_x * cells_z
    group = 8 // cells_x

    def load(j):
        part = pl.ds(j * per, per)
        return pltpu.make_async_copy(vel_hbm.at[part], vel.at[part], load_sem.at[j])

    def load_modes(k):
        src = modes_hbm.at[:, pl.ds(k * half, half)]
        return pltpu.make_async_copy(src, modes_split.at[k], load_sem.at[CHUNKS + k])

    def remote(way, j):
        part = pl.ds(j * per, per)
        rows = pl.ds(j * per * cells_x, per * cells_x)
        src, dst, where = [
            (vel_hbm.at[part, cells_x - 1], x_low.at[part], (right, gz)),
            (vel_hbm.at[part, 0], x_high.at[part], (left, gz)),
            (z_last.at[rows], z_low.at[rows], (gx, front)),
            (z_first.at[rows], z_high.at[rows], (gx, back)),
        ][way]
        return pltpu.make_async_remote_copy(
            src_ref=src, dst_ref=dst, send_sem=send_sem.at[way, j], recv_sem=recv_sem.at[way, j],
            device_id=where, device_id_type=MESH,
        )

    greet(nx, nz)
    for j in range(CHUNKS):
        load(j).start()
    for k in range(2):
        load_modes(k).start()
    pl.semaphore_wait(pltpu.get_barrier_semaphore(), nx * nz - 1)
    def send(j):
        remote(0, j).start()
        remote(1, j).start()
        load(j).wait()

        @pl.loop(j * per // group, (j + 1) * per // group)
        def _(g):
            rows = pl.ds(pl.multiple_of(g * 8, 8), 8)
            blocks = [vel[g * group + q] for q in range(group)]
            z_first[rows, :] = jnp.concatenate([b[:, 0, :] for b in blocks], axis=0)
            z_last[rows, :] = jnp.concatenate([b[:, cells_z - 1, :] for b in blocks], axis=0)

        remote(2, j).start()
        remote(3, j).start()

    for j in range(WINDOW):
        send(j)

    def gather(ref, c, count):
        parts = [ref.at[k][pl.ds(c, count, stride=cells), :] for k in range(2)]
        return jnp.concatenate(parts, axis=1)

    for k in range(2):
        load_modes(k).wait()
    for c in range(cells):
        s_ref[c, 0:modes, :] = gather(modes_split, c, modes)

    def snapshot(s):
        sub = lax.broadcasted_iota(jnp.int32, (cells_z, width), 0)
        u = [[vel[s * 3 + i, x] for x in range(cells_x)] for i in range(3)]
        low = [x_low[s * 3 + i] for i in range(3)]
        high = [x_high[s * 3 + i] for i in range(3)]
        for x in range(cells_x):
            gradx, gradz, grady = [], [], []
            for i in range(3):
                f = u[i][x]
                before = u[i][x - 1] if x > 0 else low[i]
                after = u[i][x + 1] if x < cells_x - 1 else high[i]
                gradx.append((after - before) * 0.5)
                row = pl.ds((s * 3 + i) * cells_x + x, 1)
                under = jnp.where(sub == 0, z_low[row, :], pltpu.roll(f, 1, 0))
                over = jnp.where(sub == cells_z - 1, z_high[row, :], pltpu.roll(f, cells_z - 1, 0))
                gradz.append((over - under) * 0.5)
                grady.append(lane_derivative(f))
            diagonal_part = gradx[0] * gradx[0] + gradz[1] * gradz[1] + grady[2] * grady[2]
            cross_part = gradz[0] * gradx[1] + grady[0] * gradx[2] + grady[1] * gradz[2]
            place = pl.multiple_of((s * cells_x + x) * cells_z, cells_z)
            value = -0.5 * diagonal_part - cross_part
            for k in range(2):
                crit[k, pl.ds(place, cells_z), :] = value[:, k * half : (k + 1) * half]

    few = snaps // CHUNKS
    for j in range(CHUNKS):
        for way in range(4):
            remote(way, j).wait_recv()

        @pl.loop(j * few, (j + 1) * few)
        def _(s):
            snapshot(s)

        for c in range(cells):
            got = [crit.at[k][pl.ds(j * few * cells + c, few, stride=cells), :] for k in range(2)]
            s_ref[c, modes + j * few : modes + (j + 1) * few, :] = jnp.concatenate(got, axis=1)
        for way in range(4):
            remote(way, j).wait_send()
        if j + WINDOW < CHUNKS:
            send(j + WINDOW)

    total[...] = jnp.zeros_like(total)
    columns = s_ref.shape[1]

    @pl.loop(0, cells // GROUP)
    def _(g):
        pieces = [split3(s_ref[g * GROUP + q]) for q in range(GROUP)]
        a, b, d = [jnp.concatenate(kind, axis=1) for kind in zip(*pieces)]
        total[0:columns] += dot_t(b, b)
        total[columns:] += dot_t(jnp.concatenate([a, b, d], axis=0), a)

    cross = total[2 * columns : 3 * columns] + total[3 * columns :]
    store_pieces(part, total[columns : 2 * columns] + (total[0:columns] + (cross + cross.T)))
    reduce_all(nx, nz, part, sum_ref, inbox, reduce_sems)

    factor(load_tiles(sum_ref, scale), upper_ref, inverse_ref)
    wa, wb, wc = split3(inverse_ref[...])
    main = jnp.concatenate(
        [
            jnp.concatenate([wa, wa], axis=1),
            jnp.concatenate([wb, wb], axis=1),
            jnp.concatenate([wc, jnp.zeros_like(wc)], axis=1),
        ],
        axis=0,
    )
    total[0 : 2 * columns] = jnp.zeros((2 * columns, columns), F32)

    @pl.loop(0, cells // GROUP)
    def _(g):
        tops, lows = [], []
        for q in range(GROUP):
            sa, sb, sc = split3(s_ref[g * GROUP + q])
            y = dot(main, jnp.concatenate([sa, sb], axis=0))
            x = y[0:columns] + (y[columns : 2 * columns] + y[2 * columns :] + dot(wa, sc))
            x_ref[g * GROUP + q] = x
            a, b = split2(x)
            tops.append(a)
            lows.append(b)
        a = jnp.concatenate(tops, axis=1)
        both = jnp.concatenate([a, jnp.concatenate(lows, axis=1)], axis=0)
        total[0 : 2 * columns] += dot_t(both, a)

    store = pltpu.make_async_copy(x_ref, x_hbm, load_sem.at[CHUNKS + 2])
    store.start()
    cross = total[columns : 2 * columns]
    store_pieces(part_two, total[0:columns] + (cross + cross.T))
    reduce_all(nx, nz, part_two, sum_two_ref, inbox_two, reduce_two)
    store.wait()


def halo_call(velocity, scaled_modes, nx, nz, scale):
    snaps, _, cells_x, cells_z, width = velocity.shape
    modes = scaled_modes.shape[0]
    fields = snaps * 3
    cells = cells_x * cells_z
    columns = modes + snaps
    pieces = jax.ShapeDtypeStruct((PIECES, columns // PIECES, columns), F32)
    x_face = pltpu.VMEM((fields, cells_z, width), F32)
    z_face = pltpu.VMEM((fields * cells_x, width), F32)
    return pl.pallas_call(
        functools.partial(halo_kernel, nx, nz, scale),
        out_shape=(
            jax.ShapeDtypeStruct((cells, columns, width), F32),
            pieces,
            jax.ShapeDtypeStruct((columns, columns), F32),
        ),
        in_specs=[pl.BlockSpec(memory_space=pl.ANY)] * 2,
        out_specs=[
            pl.BlockSpec(memory_space=pl.ANY),
            pl.BlockSpec(memory_space=pltpu.VMEM),
            pl.BlockSpec(memory_space=pltpu.VMEM),
        ],
        scratch_shapes=[
            pltpu.VMEM((cells, columns, width), F32),
            pltpu.VMEM((cells, columns, width), F32),
            pltpu.VMEM((columns, columns), F32),
            pltpu.VMEM(pieces.shape, F32),
            pltpu.VMEM((fields, cells_x, cells_z, width), F32),
            pltpu.VMEM((2, snaps * cells, width // 2), F32),
            pltpu.VMEM((2, modes * cells, width // 2), F32),
            x_face, x_face, z_face, z_face, z_face, z_face,
            pltpu.VMEM((4 * columns, columns), F32),
            pltpu.SemaphoreType.DMA((CHUNKS + 3,)),
            pltpu.SemaphoreType.DMA((4, CHUNKS)),
            pltpu.SemaphoreType.DMA((4, CHUNKS)),
            *reduce_scratch(nx * nz, columns),
            *reduce_scratch(nx * nz, columns),
        ],
        compiler_params=pltpu.CompilerParams(
            collective_id=0, has_side_effects=True, vmem_limit_bytes=VMEM_LIMIT
        ),
        name="halo_to_first_pass",
    )(velocity.reshape(fields, cells_x, cells_z, width), scaled_modes.reshape(modes * cells, width))


def greet(nx, nz):
    gx, gz = lax.axis_index("gx"), lax.axis_index("gz")
    barrier = pltpu.get_barrier_semaphore()
    for dx, dz in other_steps(nx, nz):
        where = (lax.rem(gx + dx, nx), lax.rem(gz + dz, nz))
        pl.semaphore_signal(barrier, inc=1, device_id=where, device_id_type=MESH)


def other_steps(nx, nz):
    return [(dx, dz) for dx in range(nx) for dz in range(nz) if dx or dz]


def reduce_all(nx, nz, part_ref, sum_ref, inbox, sems):
    send_sem, recv_sem, send_two, recv_two = [sems.at[i] for i in range(4)]
    count = nx * nz
    owners = min(count, PIECES)
    gx, gz = lax.axis_index("gx"), lax.axis_index("gz")
    me = gx * nz + gz

    def target(dx, dz):
        return lax.rem(gx + dx, nx), lax.rem(gz + dz, nz)

    def scatter(where):
        return pltpu.make_async_remote_copy(
            src_ref=part_ref.at[where[0] * nz + where[1]], dst_ref=inbox.at[me],
            send_sem=send_sem, recv_sem=recv_sem, device_id=where, device_id_type=MESH,
        )

    def spread(where):
        return pltpu.make_async_remote_copy(
            src_ref=sum_ref.at[me], dst_ref=sum_ref.at[me], send_sem=send_two, recv_sem=recv_two,
            device_id=where, device_id_type=MESH,
        )

    def wait_bytes(ref, number, sem):
        if number:
            view = ref.at[pl.ds(0, number)]
            pltpu.make_async_copy(view, view, sem).wait()

    def add_up():
        inbox[me] = part_ref[me]
        wait_bytes(inbox, count - 1, recv_sem)
        sum_ref[me] = jnp.sum(inbox[...], axis=0)

    if owners == count:
        for step in other_steps(nx, nz):
            scatter(target(*step)).start()
        add_up()
        for step in other_steps(nx, nz):
            spread(target(*step)).start()
        wait_bytes(sum_ref, count - 1, recv_two)
        wait_bytes(inbox, count - 1, send_sem)
        wait_bytes(inbox, count - 1, send_two)
    else:
        owner = me < owners

        @pl.loop(0, owners)
        def _(k):
            @pl.when(k != me)
            def _():
                scatter((lax.div(k, nz), lax.rem(k, nz))).start()

        @pl.when(owner)
        def _():
            add_up()

            @pl.loop(1, count)
            def _(step):
                k = lax.rem(me + step, count)
                spread((lax.div(k, nz), lax.rem(k, nz))).start()

            wait_bytes(sum_ref, owners - 1, recv_two)
            wait_bytes(inbox, owners - 1, send_sem)
            wait_bytes(inbox, count - 1, send_two)

        @pl.when(jnp.logical_not(owner))
        def _():
            wait_bytes(sum_ref, owners, recv_two)
            wait_bytes(inbox, owners, send_sem)


def reduce_scratch(count, columns):
    rows = columns // PIECES
    return [
        pltpu.VMEM((PIECES, rows, columns), F32),
        pltpu.VMEM((count, rows, columns), F32),
        pltpu.SemaphoreType.DMA((4,)),
    ]


def factor(tiles, upper_ref, inverse_ref):
    size = tiles[0].shape[1]
    shape = (8, size)
    lane = lax.broadcasted_iota(jnp.int32, shape, 1)
    sub = lax.broadcasted_iota(jnp.int32, shape, 0)
    for home in range(len(tiles)):
        k = home * 8
        tile = tiles[home]
        rows = [jnp.broadcast_to(tile[i : i + 1, :], shape) for i in range(8)]
        pivot = [
            [jnp.broadcast_to(rows[i][:, k + j : k + j + 1], shape) if j >= i else None for j in range(8)]
            for i in range(8)
        ]
        inv = []
        upper = jnp.zeros(shape, F32)
        inverse = jnp.zeros(shape, F32)
        for i in range(8):
            inv.append(1.0 / pivot[i][i])
            fixed = jnp.where(lane == k + i, 1.0, rows[i])
            scale = jnp.sqrt(inv[i])
            upper = jnp.where((sub == i) & (lane >= k + i), rows[i] * scale, upper)
            inverse = jnp.where((sub == i) & (lane <= k + i), fixed * scale, inverse)
            for j in range(i + 1, 8):
                ratio = pivot[i][j] * inv[i]
                rows[j] = jnp.where(lane == k + i, 0.0, rows[j]) - ratio * fixed
                for m in range(j, 8):
                    pivot[j][m] = pivot[j][m] - ratio * pivot[i][m]
            rows[i] = fixed
        upper_ref[k : k + 8, :] = upper
        inverse_ref[k : k + 8, :] = inverse
        inside = (lane >= k) & (lane < k + 8)
        clear = [jnp.where(inside & (lane > k + i), 0.0, rows[i]) for i in range(8)]
        for t in range(home + 1, len(tiles)):
            tile = tiles[t]
            new = jnp.where(inside, 0.0, tile)
            weights = []
            for i in range(8):
                entry = jnp.broadcast_to(tile[:, k + i : k + i + 1], shape)
                for m in range(i):
                    entry = entry - weights[m] * pivot[m][i]
                weights.append(entry * inv[i])
                new = new - weights[i] * clear[i]
            tiles[t] = new


def load_tiles(sum_ref, scale):
    rows = sum_ref.shape[1]
    step = 8 // rows
    return [
        jnp.concatenate([sum_ref[t * step + q] for q in range(step)], axis=0) * scale
        for t in range(sum_ref.shape[0] // step)
    ]


def second_kernel(
    scale, x_hbm, sum_ref, upper_one_ref, out_hbm, triangle_ref, lower_one_ref,
    x_ref, buffer, inverse_ref, upper_ref, load_sem, store_sem,
):
    columns, _, width = out_hbm.shape
    blocks = x_hbm.shape[0] // 8
    half = width // 2

    def load(i):
        part = pl.ds(i * 8, 8)
        return pltpu.make_async_copy(x_hbm.at[part], x_ref.at[part], load_sem.at[i])

    def store(i, k):
        where = out_hbm.at[:, pl.ds(i * 8, 8), pl.ds(k * half, half)]
        return pltpu.make_async_copy(buffer.at[i, k], where, store_sem.at[i, k])

    for i in range(blocks):
        load(i).start()
    factor(load_tiles(sum_ref, scale), upper_ref, inverse_ref)
    wa, wb = split2(inverse_ref[...])
    both = jnp.concatenate(
        [jnp.concatenate([wa, wa], axis=1), jnp.concatenate([wb, jnp.zeros_like(wb)], axis=1)],
        axis=0,
    )
    for i in range(blocks):
        load(i).wait()
        for c in range(8):
            y = dot(both, jnp.concatenate(split2(x_ref[i * 8 + c]), axis=0))
            q = y[0:columns] + y[columns:]
            for k in range(2):
                flat = buffer.at[i, k].reshape(columns * 8, half)
                flat[pl.ds(c, columns, stride=8), :] = q[:, k * half : (k + 1) * half]
        for k in range(2):
            store(i, k).start()
    lower_one_ref[...] = upper_one_ref[...].T
    triangle_ref[...] = lax.dot_general(
        upper_ref[...], upper_one_ref[...], (((1,), (0,)), ((), ())),
        precision=lax.Precision.HIGHEST, preferred_element_type=F32,
    )
    for i in range(blocks):
        for k in range(2):
            store(i, k).wait()


def shards(velocity, scaled_modes):
    snaps, _, cells_x, cells_z, width = velocity.shape
    columns = scaled_modes.shape[0] + snaps
    nx, nz = lax.axis_size("gx"), lax.axis_size("gz")
    cells = cells_x * cells_z
    scale = 1.0 / (cells * nx * nz * width)
    square = jax.ShapeDtypeStruct((columns, columns), F32)
    whole = pl.BlockSpec(memory_space=pltpu.VMEM)
    params = pltpu.CompilerParams(vmem_limit_bytes=VMEM_LIMIT)

    first_pass, sum_two, upper_one = halo_call(velocity, scaled_modes, nx, nz, scale)
    blocks = cells // 8
    basis, triangle, lower_one = pl.pallas_call(
        functools.partial(second_kernel, scale),
        out_shape=(jax.ShapeDtypeStruct((columns, cells, width), F32), square, square),
        in_specs=[pl.BlockSpec(memory_space=pl.ANY), whole, whole],
        out_specs=[pl.BlockSpec(memory_space=pl.ANY), whole, whole],
        scratch_shapes=[
            pltpu.VMEM((cells, columns, width), F32),
            pltpu.VMEM((blocks, 2, columns, 8, width // 2), F32),
            pltpu.VMEM((columns, columns), F32),
            pltpu.VMEM((columns, columns), F32),
            pltpu.SemaphoreType.DMA((blocks,)),
            pltpu.SemaphoreType.DMA((blocks, 2)),
        ],
        compiler_params=params, name="second_pass",
    )(first_pass, sum_two, upper_one)
    return (basis.reshape(columns, cells_x, cells_z, width), triangle, lower_one)


def solution(mesh):
    in_specs = (P(None, None, "gx", "gz", None), P(None, "gx", "gz", None))
    out_specs = (P(None, "gx", "gz", None), P(), P())
    return jax.shard_map(shards, mesh=mesh, in_specs=in_specs, out_specs=out_specs, check_vma=False)
```

```python
import functools

import jax
import jax.numpy as jnp
from jax import lax
from jax.experimental import pallas as pl
from jax.experimental.pallas import tpu as pltpu
from jax.sharding import PartitionSpec as P

MESH = pl.DeviceIdType.MESH
F32 = jnp.float32
BF16 = jnp.bfloat16
CHUNKS = 8
WINDOW = 3
GROUP = 8
PIECES = 32
VMEM_LIMIT = 60 * 1024 * 1024


def split3(x):
    a = x.astype(BF16)
    rest = x - a.astype(F32)
    b = rest.astype(BF16)
    c = (rest - b.astype(F32)).astype(BF16)
    return a, b, c


def split2(x):
    a = x.astype(BF16)
    return a, (x - a.astype(F32)).astype(BF16)


def dot(x, y):
    return lax.dot_general(x, y, (((1,), (0,)), ((), ())), preferred_element_type=F32)


def dot_t(x, y):
    return lax.dot_general(x, y, (((1,), (1,)), ((), ())), preferred_element_type=F32)


def store_pieces(ref, matrix):
    rows = matrix.shape[0] // PIECES
    for i in range(PIECES):
        ref[i] = matrix[i * rows : (i + 1) * rows, :]


def lane_derivative(f):
    width = f.shape[-1]
    lane = lax.broadcasted_iota(jnp.int32, f.shape, 1)
    ahead = pltpu.roll(f, width - 1, 1)
    behind = pltpu.roll(f, 1, 1)
    ahead2 = pltpu.roll(f, width - 2, 1)
    behind2 = pltpu.roll(f, 2, 1)
    inner = ahead - behind
    bottom = -3.0 * f + 4.0 * ahead - ahead2
    top_side = 3.0 * f - 4.0 * behind + behind2
    return 0.5 * jnp.where(lane == 0, bottom, jnp.where(lane == width - 1, top_side, inner))


def halo_kernel(
    nx, nz, scale, vel_hbm, modes_hbm, x_hbm, sum_two_ref, upper_ref,
    s_ref, pair_ref, third_ref, x_ref, inverse_ref, sum_ref, vel, crit, modes_split, x_low, x_high, z_low, z_high, z_first, z_last, total,
    load_sem, send_sem, recv_sem, part, inbox, reduce_sems, part_two, inbox_two, reduce_two,
):
    gx = lax.axis_index("gx")
    gz = lax.axis_index("gz")
    right, left = lax.rem(gx + 1, nx), lax.rem(gx + nx - 1, nx)
    front, back = lax.rem(gz + 1, nz), lax.rem(gz + nz - 1, nz)
    fields, cells_x, cells_z, width = vel_hbm.shape
    snaps = fields // 3
    modes = modes_hbm.shape[0] // (cells_x * cells_z)
    half = width // 2
    per = fields // CHUNKS
    cells = cells_x * cells_z
    group = 8 // cells_x

    def load(j):
        part = pl.ds(j * per, per)
        return pltpu.make_async_copy(vel_hbm.at[part], vel.at[part], load_sem.at[j])

    def load_modes(k):
        src = modes_hbm.at[:, pl.ds(k * half, half)]
        return pltpu.make_async_copy(src, modes_split.at[k], load_sem.at[CHUNKS + k])

    def remote(way, j):
        part = pl.ds(j * per, per)
        rows = pl.ds(j * per * cells_x, per * cells_x)
        src, dst, where = [
            (vel_hbm.at[part, cells_x - 1], x_low.at[part], (right, gz)),
            (vel_hbm.at[part, 0], x_high.at[part], (left, gz)),
            (z_last.at[rows], z_low.at[rows], (gx, front)),
            (z_first.at[rows], z_high.at[rows], (gx, back)),
        ][way]
        return pltpu.make_async_remote_copy(
            src_ref=src, dst_ref=dst, send_sem=send_sem.at[way, j], recv_sem=recv_sem.at[way, j],
            device_id=where, device_id_type=MESH,
        )

    greet(nx, nz)
    for j in range(CHUNKS):
        load(j).start()
    for k in range(2):
        load_modes(k).start()

    def pack(j):
        load(j).wait()

        @pl.loop(j * per // group, (j + 1) * per // group)
        def _(g):
            rows = pl.ds(pl.multiple_of(g * 8, 8), 8)
            blocks = [vel[g * group + q] for q in range(group)]
            z_first[rows, :] = jnp.concatenate([b[:, 0, :] for b in blocks], axis=0)
            z_last[rows, :] = jnp.concatenate([b[:, cells_z - 1, :] for b in blocks], axis=0)

    def send(j):
        for way in range(4):
            remote(way, j).start()

    for j in range(WINDOW):
        pack(j)
    pl.semaphore_wait(pltpu.get_barrier_semaphore(), nx * nz - 1)
    for j in range(WINDOW):
        send(j)
    for j in range(WINDOW, CHUNKS):
        pack(j)

    def gather(ref, c, count):
        parts = [ref.at[k][pl.ds(c, count, stride=cells), :] for k in range(2)]
        return jnp.concatenate(parts, axis=1)

    for k in range(2):
        load_modes(k).wait()
    for c in range(cells):
        s_ref[c, 0:modes, :] = gather(modes_split, c, modes)

    def snapshot(s):
        sub = lax.broadcasted_iota(jnp.int32, (cells_z, width), 0)
        u = [[vel[s * 3 + i, x] for x in range(cells_x)] for i in range(3)]
        low = [x_low[s * 3 + i] for i in range(3)]
        high = [x_high[s * 3 + i] for i in range(3)]
        for x in range(cells_x):
            gradx, gradz, grady = [], [], []
            for i in range(3):
                f = u[i][x]
                before = u[i][x - 1] if x > 0 else low[i]
                after = u[i][x + 1] if x < cells_x - 1 else high[i]
                gradx.append((after - before) * 0.5)
                row = pl.ds((s * 3 + i) * cells_x + x, 1)
                under = jnp.where(sub == 0, z_low[row, :], pltpu.roll(f, 1, 0))
                over = jnp.where(sub == cells_z - 1, z_high[row, :], pltpu.roll(f, cells_z - 1, 0))
                gradz.append((over - under) * 0.5)
                grady.append(lane_derivative(f))
            diagonal_part = gradx[0] * gradx[0] + gradz[1] * gradz[1] + grady[2] * grady[2]
            cross_part = gradz[0] * gradx[1] + grady[0] * gradx[2] + grady[1] * gradz[2]
            place = pl.multiple_of((s * cells_x + x) * cells_z, cells_z)
            value = -0.5 * diagonal_part - cross_part
            for k in range(2):
                crit[k, pl.ds(place, cells_z), :] = value[:, k * half : (k + 1) * half]

    few = snaps // CHUNKS
    for j in range(CHUNKS):
        for way in range(4):
            remote(way, j).wait_recv()

        @pl.loop(j * few, (j + 1) * few)
        def _(s):
            snapshot(s)

        for c in range(cells):
            got = [crit.at[k][pl.ds(j * few * cells + c, few, stride=cells), :] for k in range(2)]
            s_ref[c, modes + j * few : modes + (j + 1) * few, :] = jnp.concatenate(got, axis=1)
        for way in range(4):
            remote(way, j).wait_send()
        if j + WINDOW < CHUNKS:
            send(j + WINDOW)

    total[...] = jnp.zeros_like(total)
    columns = s_ref.shape[1]

    @pl.loop(0, cells // GROUP)
    def _(g):
        pieces = [split3(s_ref[g * GROUP + q]) for q in range(GROUP)]
        for q, (a, b, d) in enumerate(pieces):
            pair_ref[g * GROUP + q, 0:columns, :] = a
            pair_ref[g * GROUP + q, columns:, :] = b
            third_ref[g * GROUP + q] = d
        a, b, d = [jnp.concatenate(kind, axis=1) for kind in zip(*pieces)]
        total[0:columns] += dot_t(b, b)
        total[columns:] += dot_t(jnp.concatenate([a, b, d], axis=0), a)

    cross = total[2 * columns : 3 * columns] + total[3 * columns :]
    store_pieces(part, total[columns : 2 * columns] + (total[0:columns] + (cross + cross.T)))
    reduce_all(nx, nz, part, sum_ref, inbox, reduce_sems)

    factor(load_tiles(sum_ref, scale), upper_ref, inverse_ref)
    wa, wb, wc = split3(inverse_ref[...])
    main = jnp.concatenate(
        [
            jnp.concatenate([wa, wa], axis=1),
            jnp.concatenate([wb, wb], axis=1),
            jnp.concatenate([wc, jnp.zeros_like(wc)], axis=1),
        ],
        axis=0,
    )
    total[0 : 2 * columns] = jnp.zeros((2 * columns, columns), F32)

    @pl.loop(0, cells // GROUP)
    def _(g):
        tops, lows = [], []
        for q in range(GROUP):
            y = dot(main, pair_ref[g * GROUP + q])
            last = dot(wa, third_ref[g * GROUP + q])
            x = y[0:columns] + (y[columns : 2 * columns] + y[2 * columns :] + last)
            x_ref[g * GROUP + q] = x
            a, b = split2(x)
            tops.append(a)
            lows.append(b)
        a = jnp.concatenate(tops, axis=1)
        both = jnp.concatenate([a, jnp.concatenate(lows, axis=1)], axis=0)
        total[0 : 2 * columns] += dot_t(both, a)

    store = pltpu.make_async_copy(x_ref, x_hbm, load_sem.at[CHUNKS + 2])
    store.start()
    cross = total[columns : 2 * columns]
    store_pieces(part_two, total[0:columns] + (cross + cross.T))
    reduce_all(nx, nz, part_two, sum_two_ref, inbox_two, reduce_two)
    store.wait()


def halo_call(velocity, scaled_modes, nx, nz, scale):
    snaps, _, cells_x, cells_z, width = velocity.shape
    modes = scaled_modes.shape[0]
    fields = snaps * 3
    cells = cells_x * cells_z
    columns = modes + snaps
    pieces = jax.ShapeDtypeStruct((PIECES, columns // PIECES, columns), F32)
    x_face = pltpu.VMEM((fields, cells_z, width), F32)
    z_face = pltpu.VMEM((fields * cells_x, width), F32)
    return pl.pallas_call(
        functools.partial(halo_kernel, nx, nz, scale),
        out_shape=(
            jax.ShapeDtypeStruct((cells, columns, width), F32),
            pieces,
            jax.ShapeDtypeStruct((columns, columns), F32),
        ),
        in_specs=[pl.BlockSpec(memory_space=pl.ANY)] * 2,
        out_specs=[
            pl.BlockSpec(memory_space=pl.ANY),
            pl.BlockSpec(memory_space=pltpu.VMEM),
            pl.BlockSpec(memory_space=pltpu.VMEM),
        ],
        scratch_shapes=[
            pltpu.VMEM((cells, columns, width), F32),
            pltpu.VMEM((cells, 2 * columns, width), BF16),
            pltpu.VMEM((cells, columns, width), BF16),
            pltpu.VMEM((cells, columns, width), F32),
            pltpu.VMEM((columns, columns), F32),
            pltpu.VMEM(pieces.shape, F32),
            pltpu.VMEM((fields, cells_x, cells_z, width), F32),
            pltpu.VMEM((2, snaps * cells, width // 2), F32),
            pltpu.VMEM((2, modes * cells, width // 2), F32),
            x_face, x_face, z_face, z_face, z_face, z_face,
            pltpu.VMEM((4 * columns, columns), F32),
            pltpu.SemaphoreType.DMA((CHUNKS + 3,)),
            pltpu.SemaphoreType.DMA((4, CHUNKS)),
            pltpu.SemaphoreType.DMA((4, CHUNKS)),
            *reduce_scratch(nx * nz, columns),
            *reduce_scratch(nx * nz, columns),
        ],
        compiler_params=pltpu.CompilerParams(
            collective_id=0, has_side_effects=True, vmem_limit_bytes=VMEM_LIMIT
        ),
        name="halo_to_first_pass",
    )(velocity.reshape(fields, cells_x, cells_z, width), scaled_modes.reshape(modes * cells, width))


def greet(nx, nz):
    gx, gz = lax.axis_index("gx"), lax.axis_index("gz")
    barrier = pltpu.get_barrier_semaphore()
    for dx, dz in other_steps(nx, nz):
        where = (lax.rem(gx + dx, nx), lax.rem(gz + dz, nz))
        pl.semaphore_signal(barrier, inc=1, device_id=where, device_id_type=MESH)


def other_steps(nx, nz):
    return [(dx, dz) for dx in range(nx) for dz in range(nz) if dx or dz]


def reduce_all(nx, nz, part_ref, sum_ref, inbox, sems):
    send_sem, recv_sem, send_two, recv_two = [sems.at[i] for i in range(4)]
    count = nx * nz
    owners = min(count, PIECES)
    gx, gz = lax.axis_index("gx"), lax.axis_index("gz")
    me = gx * nz + gz

    def target(dx, dz):
        return lax.rem(gx + dx, nx), lax.rem(gz + dz, nz)

    def scatter(where):
        return pltpu.make_async_remote_copy(
            src_ref=part_ref.at[where[0] * nz + where[1]], dst_ref=inbox.at[me],
            send_sem=send_sem, recv_sem=recv_sem, device_id=where, device_id_type=MESH,
        )

    def spread(where):
        return pltpu.make_async_remote_copy(
            src_ref=sum_ref.at[me], dst_ref=sum_ref.at[me], send_sem=send_two, recv_sem=recv_two,
            device_id=where, device_id_type=MESH,
        )

    def wait_bytes(ref, number, sem):
        if number:
            view = ref.at[pl.ds(0, number)]
            pltpu.make_async_copy(view, view, sem).wait()

    def add_up():
        inbox[me] = part_ref[me]
        wait_bytes(inbox, count - 1, recv_sem)
        sum_ref[me] = jnp.sum(inbox[...], axis=0)

    if owners == count:
        for step in other_steps(nx, nz):
            scatter(target(*step)).start()
        add_up()
        for step in other_steps(nx, nz):
            spread(target(*step)).start()
        wait_bytes(sum_ref, count - 1, recv_two)
        wait_bytes(inbox, count - 1, send_sem)
        wait_bytes(inbox, count - 1, send_two)
    else:
        owner = me < owners

        @pl.loop(0, owners)
        def _(k):
            @pl.when(k != me)
            def _():
                scatter((lax.div(k, nz), lax.rem(k, nz))).start()

        @pl.when(owner)
        def _():
            add_up()

            @pl.loop(1, count)
            def _(step):
                k = lax.rem(me + step, count)
                spread((lax.div(k, nz), lax.rem(k, nz))).start()

            wait_bytes(sum_ref, owners - 1, recv_two)
            wait_bytes(inbox, owners - 1, send_sem)
            wait_bytes(inbox, count - 1, send_two)

        @pl.when(jnp.logical_not(owner))
        def _():
            wait_bytes(sum_ref, owners, recv_two)
            wait_bytes(inbox, owners, send_sem)


def reduce_scratch(count, columns):
    rows = columns // PIECES
    return [
        pltpu.VMEM((PIECES, rows, columns), F32),
        pltpu.VMEM((count, rows, columns), F32),
        pltpu.SemaphoreType.DMA((4,)),
    ]


def factor(tiles, upper_ref, inverse_ref):
    size = tiles[0].shape[1]
    shape = (8, size)
    lane = lax.broadcasted_iota(jnp.int32, shape, 1)
    sub = lax.broadcasted_iota(jnp.int32, shape, 0)
    marks = [lane == sub + 8 * t for t in range(len(tiles))]
    found = jnp.zeros(shape, F32)
    for mark, tile in zip(marks, tiles):
        found = jnp.where(mark, tile, found)
    diagonal = jnp.broadcast_to(jnp.sum(found, axis=0, keepdims=True), shape)
    shrink = 1.0 / jnp.sqrt(diagonal)
    grow = diagonal * shrink
    for t, mark in enumerate(marks):
        side = jnp.sum(jnp.where(mark, shrink, 0.0), axis=1, keepdims=True)
        tiles[t] = tiles[t] * jnp.broadcast_to(side, shape) * shrink
    for home in range(len(tiles)):
        k = home * 8
        tile = tiles[home]
        rows = [jnp.broadcast_to(tile[i : i + 1, :], shape) for i in range(8)]
        pivot = [
            [jnp.broadcast_to(rows[i][:, k + j : k + j + 1], shape) if j >= i else None for j in range(8)]
            for i in range(8)
        ]
        inv = []
        upper = jnp.zeros(shape, F32)
        inverse = jnp.zeros(shape, F32)
        for i in range(8):
            if i % 2 == 0:
                one, both, two = pivot[i][i], pivot[i][i + 1], pivot[i + 1][i + 1]
                inv.append(1.0 / one)
                inv.append(one * (1.0 / (one * two - both * both)))
            fixed = jnp.where(lane == k + i, 1.0, rows[i])
            scale = jnp.sqrt(inv[i])
            upper = jnp.where((sub == i) & (lane >= k + i), rows[i] * scale, upper)
            inverse = jnp.where((sub == i) & (lane <= k + i), fixed * scale, inverse)
            for j in range(i + 1, 8):
                ratio = pivot[i][j] * inv[i]
                rows[j] = jnp.where(lane == k + i, 0.0, rows[j]) - ratio * fixed
                for m in range(j, 8):
                    pivot[j][m] = pivot[j][m] - ratio * pivot[i][m]
            rows[i] = fixed
        upper_ref[k : k + 8, :] = upper * grow
        inverse_ref[k : k + 8, :] = inverse * shrink
        inside = (lane >= k) & (lane < k + 8)
        clear = [jnp.where(inside & (lane > k + i), 0.0, rows[i]) for i in range(8)]
        for t in range(home + 1, len(tiles)):
            tile = tiles[t]
            new = jnp.where(inside, 0.0, tile)
            weights = []
            for i in range(8):
                entry = jnp.broadcast_to(tile[:, k + i : k + i + 1], shape)
                for m in range(i):
                    entry = entry - weights[m] * pivot[m][i]
                weights.append(entry * inv[i])
                new = new - weights[i] * clear[i]
            tiles[t] = new


def load_tiles(sum_ref, scale):
    rows = sum_ref.shape[1]
    step = 8 // rows
    return [
        jnp.concatenate([sum_ref[t * step + q] for q in range(step)], axis=0) * scale
        for t in range(sum_ref.shape[0] // step)
    ]


def second_kernel(
    scale, x_hbm, sum_ref, upper_one_ref, out_hbm, triangle_ref, lower_one_ref,
    x_ref, buffer, inverse_ref, upper_ref, load_sem, store_sem,
):
    columns, _, width = out_hbm.shape
    blocks = x_hbm.shape[0] // 8
    half = width // 2

    def load(i):
        part = pl.ds(i * 8, 8)
        return pltpu.make_async_copy(x_hbm.at[part], x_ref.at[part], load_sem.at[i])

    def store(i, k):
        where = out_hbm.at[:, pl.ds(i * 8, 8), pl.ds(k * half, half)]
        return pltpu.make_async_copy(buffer.at[i, k], where, store_sem.at[i, k])

    for i in range(blocks):
        load(i).start()
    factor(load_tiles(sum_ref, scale), upper_ref, inverse_ref)
    wa, wb = split2(inverse_ref[...])
    both = jnp.concatenate(
        [jnp.concatenate([wa, wa], axis=1), jnp.concatenate([wb, jnp.zeros_like(wb)], axis=1)],
        axis=0,
    )
    for i in range(blocks):
        load(i).wait()
        for c in range(8):
            y = dot(both, jnp.concatenate(split2(x_ref[i * 8 + c]), axis=0))
            q = y[0:columns] + y[columns:]
            for k in range(2):
                flat = buffer.at[i, k].reshape(columns * 8, half)
                flat[pl.ds(c, columns, stride=8), :] = q[:, k * half : (k + 1) * half]
        for k in range(2):
            store(i, k).start()
    lower_one_ref[...] = upper_one_ref[...].T
    triangle_ref[...] = lax.dot_general(
        upper_ref[...], upper_one_ref[...], (((1,), (0,)), ((), ())),
        precision=lax.Precision.HIGHEST, preferred_element_type=F32,
    )
    for i in range(blocks):
        for k in range(2):
            store(i, k).wait()


def shards(velocity, scaled_modes):
    snaps, _, cells_x, cells_z, width = velocity.shape
    columns = scaled_modes.shape[0] + snaps
    nx, nz = lax.axis_size("gx"), lax.axis_size("gz")
    cells = cells_x * cells_z
    scale = 1.0 / (cells * nx * nz * width)
    square = jax.ShapeDtypeStruct((columns, columns), F32)
    whole = pl.BlockSpec(memory_space=pltpu.VMEM)
    params = pltpu.CompilerParams(vmem_limit_bytes=VMEM_LIMIT)

    first_pass, sum_two, upper_one = halo_call(velocity, scaled_modes, nx, nz, scale)
    blocks = cells // 8
    basis, triangle, lower_one = pl.pallas_call(
        functools.partial(second_kernel, scale),
        out_shape=(jax.ShapeDtypeStruct((columns, cells, width), F32), square, square),
        in_specs=[pl.BlockSpec(memory_space=pl.ANY), whole, whole],
        out_specs=[pl.BlockSpec(memory_space=pl.ANY), whole, whole],
        scratch_shapes=[
            pltpu.VMEM((cells, columns, width), F32),
            pltpu.VMEM((blocks, 2, columns, 8, width // 2), F32),
            pltpu.VMEM((columns, columns), F32),
            pltpu.VMEM((columns, columns), F32),
            pltpu.SemaphoreType.DMA((blocks,)),
            pltpu.SemaphoreType.DMA((blocks, 2)),
        ],
        compiler_params=params, name="second_pass",
    )(first_pass, sum_two, upper_one)
    return (basis.reshape(columns, cells_x, cells_z, width), triangle, lower_one)


def solution(mesh):
    in_specs = (P(None, None, "gx", "gz", None), P(None, "gx", "gz", None))
    out_specs = (P(None, "gx", "gz", None), P(), P())
    return jax.shard_map(shards, mesh=mesh, in_specs=in_specs, out_specs=out_specs, check_vma=False)
```

```python
import functools

import jax
import jax.numpy as jnp
from jax import lax
from jax.experimental import pallas as pl
from jax.experimental.pallas import tpu as pltpu
from jax.sharding import PartitionSpec as P

MESH = pl.DeviceIdType.MESH
F32 = jnp.float32
BF16 = jnp.bfloat16
CHUNKS = 8
WINDOW = 8
GROUP = 16
PIECES = 32
VMEM_LIMIT = 60 * 1024 * 1024


def split3(x):
    a = x.astype(BF16)
    rest = x - a.astype(F32)
    b = rest.astype(BF16)
    c = (rest - b.astype(F32)).astype(BF16)
    return a, b, c


def split2(x):
    a = x.astype(BF16)
    return a, (x - a.astype(F32)).astype(BF16)


def dot(x, y):
    return lax.dot_general(x, y, (((1,), (0,)), ((), ())), preferred_element_type=F32)


def dot_t(x, y):
    return lax.dot_general(x, y, (((1,), (1,)), ((), ())), preferred_element_type=F32)


def store_pieces(ref, matrix):
    rows = matrix.shape[0] // PIECES
    for i in range(PIECES):
        ref[i] = matrix[i * rows : (i + 1) * rows, :]


def lane_derivative(f):
    width = f.shape[-1]
    lane = lax.broadcasted_iota(jnp.int32, f.shape, 1)
    ahead = pltpu.roll(f, width - 1, 1)
    behind = pltpu.roll(f, 1, 1)
    ahead2 = pltpu.roll(f, width - 2, 1)
    behind2 = pltpu.roll(f, 2, 1)
    inner = ahead - behind
    bottom = -3.0 * f + 4.0 * ahead - ahead2
    top_side = 3.0 * f - 4.0 * behind + behind2
    return 0.5 * jnp.where(lane == 0, bottom, jnp.where(lane == width - 1, top_side, inner))


def halo_kernel(
    nx, nz, scale, vel_hbm, modes_hbm, x_hbm, sum_two_ref, upper_ref,
    s_ref, pair_ref, third_ref, x_ref, inverse_ref, sum_ref, vel, crit, modes_split, x_low, x_high, z_low, z_high, z_first, z_last, total,
    load_sem, send_sem, recv_sem, part, inbox, reduce_sems, part_two, inbox_two, reduce_two,
):
    gx = lax.axis_index("gx")
    gz = lax.axis_index("gz")
    right, left = lax.rem(gx + 1, nx), lax.rem(gx + nx - 1, nx)
    front, back = lax.rem(gz + 1, nz), lax.rem(gz + nz - 1, nz)
    fields, cells_x, cells_z, width = vel_hbm.shape
    snaps = fields // 3
    modes = modes_hbm.shape[0] // (cells_x * cells_z)
    half = width // 2
    per = fields // CHUNKS
    cells = cells_x * cells_z
    group = 8 // cells_x

    def load(j):
        part = pl.ds(j * per, per)
        return pltpu.make_async_copy(vel_hbm.at[part], vel.at[part], load_sem.at[j])

    def load_modes(k):
        src = modes_hbm.at[:, pl.ds(k * half, half)]
        return pltpu.make_async_copy(src, modes_split.at[k], load_sem.at[CHUNKS + k])

    def remote(way, j):
        part = pl.ds(j * per, per)
        rows = pl.ds(j * per * cells_x, per * cells_x)
        src, dst, where = [
            (vel_hbm.at[part, cells_x - 1], x_low.at[part], (right, gz)),
            (vel_hbm.at[part, 0], x_high.at[part], (left, gz)),
            (z_last.at[rows], z_low.at[rows], (gx, front)),
            (z_first.at[rows], z_high.at[rows], (gx, back)),
        ][way]
        return pltpu.make_async_remote_copy(
            src_ref=src, dst_ref=dst, send_sem=send_sem.at[way, j], recv_sem=recv_sem.at[way, j],
            device_id=where, device_id_type=MESH,
        )

    greet(nx, nz)
    for j in range(CHUNKS):
        load(j).start()
    for k in range(2):
        load_modes(k).start()

    def pack(j):
        load(j).wait()

        @pl.loop(j * per // group, (j + 1) * per // group)
        def _(g):
            rows = pl.ds(pl.multiple_of(g * 8, 8), 8)
            blocks = [vel[g * group + q] for q in range(group)]
            z_first[rows, :] = jnp.concatenate([b[:, 0, :] for b in blocks], axis=0)
            z_last[rows, :] = jnp.concatenate([b[:, cells_z - 1, :] for b in blocks], axis=0)

    def send(j):
        for way in range(4):
            remote(way, j).start()

    for j in range(WINDOW):
        pack(j)
    pl.semaphore_wait(pltpu.get_barrier_semaphore(), nx * nz - 1)
    for j in range(WINDOW):
        send(j)
    for j in range(WINDOW, CHUNKS):
        pack(j)

    def gather(ref, c, count):
        parts = [ref.at[k][pl.ds(c, count, stride=cells), :] for k in range(2)]
        return jnp.concatenate(parts, axis=1)

    for k in range(2):
        load_modes(k).wait()
    for c in range(cells):
        s_ref[c, 0:modes, :] = gather(modes_split, c, modes)

    def snapshot(s):
        sub = lax.broadcasted_iota(jnp.int32, (cells_z, width), 0)
        u = [[vel[s * 3 + i, x] for x in range(cells_x)] for i in range(3)]
        low = [x_low[s * 3 + i] for i in range(3)]
        high = [x_high[s * 3 + i] for i in range(3)]
        for x in range(cells_x):
            gradx, gradz, grady = [], [], []
            for i in range(3):
                f = u[i][x]
                before = u[i][x - 1] if x > 0 else low[i]
                after = u[i][x + 1] if x < cells_x - 1 else high[i]
                gradx.append((after - before) * 0.5)
                row = pl.ds((s * 3 + i) * cells_x + x, 1)
                under = jnp.where(sub == 0, z_low[row, :], pltpu.roll(f, 1, 0))
                over = jnp.where(sub == cells_z - 1, z_high[row, :], pltpu.roll(f, cells_z - 1, 0))
                gradz.append((over - under) * 0.5)
                grady.append(lane_derivative(f))
            diagonal_part = gradx[0] * gradx[0] + gradz[1] * gradz[1] + grady[2] * grady[2]
            cross_part = gradz[0] * gradx[1] + grady[0] * gradx[2] + grady[1] * gradz[2]
            place = pl.multiple_of((s * cells_x + x) * cells_z, cells_z)
            value = -0.5 * diagonal_part - cross_part
            for k in range(2):
                crit[k, pl.ds(place, cells_z), :] = value[:, k * half : (k + 1) * half]

    few = snaps // CHUNKS
    for j in range(CHUNKS):
        for way in range(4):
            remote(way, j).wait_recv()

        @pl.loop(j * few, (j + 1) * few)
        def _(s):
            snapshot(s)

        for c in range(cells):
            got = [crit.at[k][pl.ds(j * few * cells + c, few, stride=cells), :] for k in range(2)]
            s_ref[c, modes + j * few : modes + (j + 1) * few, :] = jnp.concatenate(got, axis=1)
        for way in range(4):
            remote(way, j).wait_send()
        if j + WINDOW < CHUNKS:
            send(j + WINDOW)

    total[...] = jnp.zeros_like(total)
    columns = s_ref.shape[1]

    @pl.loop(0, cells // GROUP)
    def _(g):
        pieces = [split3(s_ref[g * GROUP + q]) for q in range(GROUP)]
        for q, (a, b, d) in enumerate(pieces):
            pair_ref[g * GROUP + q, 0:columns, :] = a
            pair_ref[g * GROUP + q, columns:, :] = b
            third_ref[g * GROUP + q] = d
        a, b, d = [jnp.concatenate(kind, axis=1) for kind in zip(*pieces)]
        total[0:columns] += dot_t(b, b)
        total[columns:] += dot_t(jnp.concatenate([a, b, d], axis=0), a)

    cross = total[2 * columns : 3 * columns] + total[3 * columns :]
    store_pieces(part, total[columns : 2 * columns] + (total[0:columns] + (cross + cross.T)))
    reduce_all(nx, nz, part, sum_ref, inbox, reduce_sems)

    factor(load_tiles(sum_ref, scale), upper_ref, inverse_ref)
    wa, wb, wc = split3(inverse_ref[...])
    main = jnp.concatenate(
        [
            jnp.concatenate([wa, wa], axis=1),
            jnp.concatenate([wb, wb], axis=1),
            jnp.concatenate([wc, jnp.zeros_like(wc)], axis=1),
        ],
        axis=0,
    )
    total[0 : 2 * columns] = jnp.zeros((2 * columns, columns), F32)

    @pl.loop(0, cells // GROUP)
    def _(g):
        tops, lows = [], []
        for q in range(GROUP):
            y = dot(main, pair_ref[g * GROUP + q])
            last = dot(wa, third_ref[g * GROUP + q])
            x = y[0:columns] + (y[columns : 2 * columns] + y[2 * columns :] + last)
            x_ref[g * GROUP + q] = x
            a, b = split2(x)
            tops.append(a)
            lows.append(b)
        a = jnp.concatenate(tops, axis=1)
        both = jnp.concatenate([a, jnp.concatenate(lows, axis=1)], axis=0)
        total[0 : 2 * columns] += dot_t(both, a)

    store = pltpu.make_async_copy(x_ref, x_hbm, load_sem.at[CHUNKS + 2])
    store.start()
    cross = total[columns : 2 * columns]
    store_pieces(part_two, total[0:columns] + (cross + cross.T))
    reduce_all(nx, nz, part_two, sum_two_ref, inbox_two, reduce_two)
    store.wait()


def halo_call(velocity, scaled_modes, nx, nz, scale):
    snaps, _, cells_x, cells_z, width = velocity.shape
    modes = scaled_modes.shape[0]
    fields = snaps * 3
    cells = cells_x * cells_z
    columns = modes + snaps
    pieces = jax.ShapeDtypeStruct((PIECES, columns // PIECES, columns), F32)
    x_face = pltpu.VMEM((fields, cells_z, width), F32)
    z_face = pltpu.VMEM((fields * cells_x, width), F32)
    return pl.pallas_call(
        functools.partial(halo_kernel, nx, nz, scale),
        out_shape=(
            jax.ShapeDtypeStruct((cells, columns, width), F32),
            pieces,
            jax.ShapeDtypeStruct((columns, columns), F32),
        ),
        in_specs=[pl.BlockSpec(memory_space=pl.ANY)] * 2,
        out_specs=[
            pl.BlockSpec(memory_space=pl.ANY),
            pl.BlockSpec(memory_space=pltpu.VMEM),
            pl.BlockSpec(memory_space=pltpu.VMEM),
        ],
        scratch_shapes=[
            pltpu.VMEM((cells, columns, width), F32),
            pltpu.VMEM((cells, 2 * columns, width), BF16),
            pltpu.VMEM((cells, columns, width), BF16),
            pltpu.VMEM((cells, columns, width), F32),
            pltpu.VMEM((columns, columns), F32),
            pltpu.VMEM(pieces.shape, F32),
            pltpu.VMEM((fields, cells_x, cells_z, width), F32),
            pltpu.VMEM((2, snaps * cells, width // 2), F32),
            pltpu.VMEM((2, modes * cells, width // 2), F32),
            x_face, x_face, z_face, z_face, z_face, z_face,
            pltpu.VMEM((4 * columns, columns), F32),
            pltpu.SemaphoreType.DMA((CHUNKS + 3,)),
            pltpu.SemaphoreType.DMA((4, CHUNKS)),
            pltpu.SemaphoreType.DMA((4, CHUNKS)),
            *reduce_scratch(nx * nz, columns),
            *reduce_scratch(nx * nz, columns),
        ],
        compiler_params=pltpu.CompilerParams(
            collective_id=0, has_side_effects=True, vmem_limit_bytes=VMEM_LIMIT
        ),
        name="halo_to_first_pass",
    )(velocity.reshape(fields, cells_x, cells_z, width), scaled_modes.reshape(modes * cells, width))


def greet(nx, nz):
    gx, gz = lax.axis_index("gx"), lax.axis_index("gz")
    barrier = pltpu.get_barrier_semaphore()
    for dx, dz in other_steps(nx, nz):
        where = (lax.rem(gx + dx, nx), lax.rem(gz + dz, nz))
        pl.semaphore_signal(barrier, inc=1, device_id=where, device_id_type=MESH)


def other_steps(nx, nz):
    return [(dx, dz) for dx in range(nx) for dz in range(nz) if dx or dz]


def reduce_all(nx, nz, part_ref, sum_ref, inbox, sems):
    send_sem, recv_sem, send_two, recv_two = [sems.at[i] for i in range(4)]
    count = nx * nz
    owners = min(count, PIECES)
    gx, gz = lax.axis_index("gx"), lax.axis_index("gz")
    me = gx * nz + gz

    def target(dx, dz):
        return lax.rem(gx + dx, nx), lax.rem(gz + dz, nz)

    def scatter(where):
        return pltpu.make_async_remote_copy(
            src_ref=part_ref.at[where[0] * nz + where[1]], dst_ref=inbox.at[me],
            send_sem=send_sem, recv_sem=recv_sem, device_id=where, device_id_type=MESH,
        )

    def spread(where):
        return pltpu.make_async_remote_copy(
            src_ref=sum_ref.at[me], dst_ref=sum_ref.at[me], send_sem=send_two, recv_sem=recv_two,
            device_id=where, device_id_type=MESH,
        )

    def wait_bytes(ref, number, sem):
        if number:
            view = ref.at[pl.ds(0, number)]
            pltpu.make_async_copy(view, view, sem).wait()

    def add_up():
        inbox[me] = part_ref[me]
        wait_bytes(inbox, count - 1, recv_sem)
        sum_ref[me] = jnp.sum(inbox[...], axis=0)

    if owners == count:
        for step in other_steps(nx, nz):
            scatter(target(*step)).start()
        add_up()
        for step in other_steps(nx, nz):
            spread(target(*step)).start()
        wait_bytes(sum_ref, count - 1, recv_two)
        wait_bytes(inbox, count - 1, send_sem)
        wait_bytes(inbox, count - 1, send_two)
    else:
        owner = me < owners

        @pl.loop(0, owners)
        def _(k):
            @pl.when(k != me)
            def _():
                scatter((lax.div(k, nz), lax.rem(k, nz))).start()

        @pl.when(owner)
        def _():
            add_up()

            @pl.loop(1, count)
            def _(step):
                k = lax.rem(me + step, count)
                spread((lax.div(k, nz), lax.rem(k, nz))).start()

            wait_bytes(sum_ref, owners - 1, recv_two)
            wait_bytes(inbox, owners - 1, send_sem)
            wait_bytes(inbox, count - 1, send_two)

        @pl.when(jnp.logical_not(owner))
        def _():
            wait_bytes(sum_ref, owners, recv_two)
            wait_bytes(inbox, owners, send_sem)


def reduce_scratch(count, columns):
    rows = columns // PIECES
    return [
        pltpu.VMEM((PIECES, rows, columns), F32),
        pltpu.VMEM((count, rows, columns), F32),
        pltpu.SemaphoreType.DMA((4,)),
    ]


def factor(tiles, upper_ref, inverse_ref):
    size = tiles[0].shape[1]
    shape = (8, size)
    lane = lax.broadcasted_iota(jnp.int32, shape, 1)
    sub = lax.broadcasted_iota(jnp.int32, shape, 0)
    marks = [lane == sub + 8 * t for t in range(len(tiles))]
    found = jnp.zeros(shape, F32)
    for mark, tile in zip(marks, tiles):
        found = jnp.where(mark, tile, found)
    diagonal = jnp.broadcast_to(jnp.sum(found, axis=0, keepdims=True), shape)
    shrink = 1.0 / jnp.sqrt(diagonal)
    grow = diagonal * shrink
    for t, mark in enumerate(marks):
        side = jnp.sum(jnp.where(mark, shrink, 0.0), axis=1, keepdims=True)
        tiles[t] = tiles[t] * jnp.broadcast_to(side, shape) * shrink
    for home in range(len(tiles)):
        k = home * 8
        tile = tiles[home]
        rows = [jnp.broadcast_to(tile[i : i + 1, :], shape) for i in range(8)]
        pivot = [
            [jnp.broadcast_to(rows[i][:, k + j : k + j + 1], shape) if j >= i else None for j in range(8)]
            for i in range(8)
        ]
        inv = []
        upper = jnp.zeros(shape, F32)
        inverse = jnp.zeros(shape, F32)
        for i in range(8):
            if i % 2 == 0:
                one, both, two = pivot[i][i], pivot[i][i + 1], pivot[i + 1][i + 1]
                inv.append(1.0 / one)
                inv.append(one * (1.0 / (one * two - both * both)))
            fixed = jnp.where(lane == k + i, 1.0, rows[i])
            scale = jnp.sqrt(inv[i])
            upper = jnp.where((sub == i) & (lane >= k + i), rows[i] * scale, upper)
            inverse = jnp.where((sub == i) & (lane <= k + i), fixed * scale, inverse)
            for j in range(i + 1, 8):
                ratio = pivot[i][j] * inv[i]
                rows[j] = jnp.where(lane == k + i, 0.0, rows[j]) - ratio * fixed
                for m in range(j, 8):
                    pivot[j][m] = pivot[j][m] - ratio * pivot[i][m]
            rows[i] = fixed
        upper_ref[k : k + 8, :] = upper * grow
        inverse_ref[k : k + 8, :] = inverse * shrink
        inside = (lane >= k) & (lane < k + 8)
        clear = [jnp.where(inside & (lane > k + i), 0.0, rows[i]) for i in range(8)]
        for t in range(home + 1, len(tiles)):
            tile = tiles[t]
            new = jnp.where(inside, 0.0, tile)
            weights = []
            for i in range(8):
                entry = jnp.broadcast_to(tile[:, k + i : k + i + 1], shape)
                for m in range(i):
                    entry = entry - weights[m] * pivot[m][i]
                weights.append(entry * inv[i])
                new = new - weights[i] * clear[i]
            tiles[t] = new


def load_tiles(sum_ref, scale):
    rows = sum_ref.shape[1]
    step = 8 // rows
    return [
        jnp.concatenate([sum_ref[t * step + q] for q in range(step)], axis=0) * scale
        for t in range(sum_ref.shape[0] // step)
    ]


def second_kernel(
    scale, x_hbm, sum_ref, upper_one_ref, out_hbm, triangle_ref, lower_one_ref,
    x_ref, buffer, inverse_ref, upper_ref, load_sem, store_sem,
):
    columns, _, width = out_hbm.shape
    blocks = x_hbm.shape[0] // 8
    half = width // 2

    def load(i):
        part = pl.ds(i * 8, 8)
        return pltpu.make_async_copy(x_hbm.at[part], x_ref.at[part], load_sem.at[i])

    def store(i, k):
        where = out_hbm.at[:, pl.ds(i * 8, 8), pl.ds(k * half, half)]
        return pltpu.make_async_copy(buffer.at[i, k], where, store_sem.at[i, k])

    for i in range(blocks):
        load(i).start()
    factor(load_tiles(sum_ref, scale), upper_ref, inverse_ref)
    wa, wb = split2(inverse_ref[...])
    both = jnp.concatenate(
        [jnp.concatenate([wa, wa], axis=1), jnp.concatenate([wb, jnp.zeros_like(wb)], axis=1)],
        axis=0,
    )
    for i in range(blocks):
        load(i).wait()
        for c in range(8):
            y = dot(both, jnp.concatenate(split2(x_ref[i * 8 + c]), axis=0))
            q = y[0:columns] + y[columns:]
            for k in range(2):
                flat = buffer.at[i, k].reshape(columns * 8, half)
                flat[pl.ds(c, columns, stride=8), :] = q[:, k * half : (k + 1) * half]
        for k in range(2):
            store(i, k).start()
    lower_one_ref[...] = upper_one_ref[...].T
    triangle_ref[...] = lax.dot_general(
        upper_ref[...], upper_one_ref[...], (((1,), (0,)), ((), ())),
        precision=lax.Precision.HIGHEST, preferred_element_type=F32,
    )
    for i in range(blocks):
        for k in range(2):
            store(i, k).wait()


def shards(velocity, scaled_modes):
    snaps, _, cells_x, cells_z, width = velocity.shape
    columns = scaled_modes.shape[0] + snaps
    nx, nz = lax.axis_size("gx"), lax.axis_size("gz")
    cells = cells_x * cells_z
    scale = 1.0 / (cells * nx * nz * width)
    square = jax.ShapeDtypeStruct((columns, columns), F32)
    whole = pl.BlockSpec(memory_space=pltpu.VMEM)
    params = pltpu.CompilerParams(vmem_limit_bytes=VMEM_LIMIT)

    first_pass, sum_two, upper_one = halo_call(velocity, scaled_modes, nx, nz, scale)
    blocks = cells // 8
    basis, triangle, lower_one = pl.pallas_call(
        functools.partial(second_kernel, scale),
        out_shape=(jax.ShapeDtypeStruct((columns, cells, width), F32), square, square),
        in_specs=[pl.BlockSpec(memory_space=pl.ANY), whole, whole],
        out_specs=[pl.BlockSpec(memory_space=pl.ANY), whole, whole],
        scratch_shapes=[
            pltpu.VMEM((cells, columns, width), F32),
            pltpu.VMEM((blocks, 2, columns, 8, width // 2), F32),
            pltpu.VMEM((columns, columns), F32),
            pltpu.VMEM((columns, columns), F32),
            pltpu.SemaphoreType.DMA((blocks,)),
            pltpu.SemaphoreType.DMA((blocks, 2)),
        ],
        compiler_params=params, name="second_pass",
    )(first_pass, sum_two, upper_one)
    return (basis.reshape(columns, cells_x, cells_z, width), triangle, lower_one)


def solution(mesh):
    in_specs = (P(None, None, "gx", "gz", None), P(None, "gx", "gz", None))
    out_specs = (P(None, "gx", "gz", None), P(), P())
    return jax.shard_map(shards, mesh=mesh, in_specs=in_specs, out_specs=out_specs, check_vma=False)
```
